32 devices in a mesh: row: 4 (over x, core), col: 8 (over z, y).
Axes of the slice: x: 2, y: 2, z: 4, core: 2. Of those that a mesh axis runs over, the one named last changes fastest.
Arguments:
- hidden: bfloat16 [512, 3584], P(('row', 'col')), may hold values from -6 to 6
- route_ids: int32 [512, 8], P(('row', 'col')), may hold values from 0 to 31, all different within a row; in each aligned block of 16 rows (0 to 15, 16 to 31, ...) at most 8 rows name the same one
- route_scores: float32 [512, 8], P(('row', 'col')), may hold values from 0.05 to 1
- gate_weight: bfloat16 [32, 3584, 1024], P(('row', 'col')), may hold values from -0.09375 to 0.09375
- up_weight: bfloat16 [32, 3584, 1024], P(('row', 'col')), may hold values from -0.09375 to 0.09375
- down_weight: bfloat16 [32, 1024, 3584], P(('row', 'col')), may hold values from -0.1875 to 0.1875
- queries: bfloat16 [512, 64, 576], P(('row', 'col'))
- latent_cache: bfloat16 [512, 128, 576], P(('row', 'col'))
- lengths: int32 [512], P(('row', 'col')), may hold values from 1 to 128, 32768 in all
Outputs:
- expert_mix: bfloat16 [512, 3584], P(('row', 'col'))
- context: bfloat16 [512, 64, 512], P(('row', 'col'))
The draws below stay inside these ranges and needn't reach their ends.
Inputs may be any that keep to these rules, and one draw needn't show every extreme that they name: `route_ids`: among the 16 sequences of one device (aligned blocks of rows), no expert is named more than 8 times, and in every draw some expert is named exactly 8 times; each row names 8 different experts. `lengths`: some sequence fills all 128 slots.
All inputs are finite; a program needn't handle non-finite values. No bound on the sum of `lengths` on one device may be relied on, other than what follows from the above.
Results may differ from the reference program's by a relative error of at most 0.013.
Values may be sent and summed in bfloat16 or wider, within the bound.
A program may use at most 128 MiB of HBM per device.

```python
import math
import jax
import jax.numpy as jnp
import numpy as np
from jax import lax

D = 3584
FF = 1024
HEADS = 64
LATENT = 512
ROPE = 64
CACHE = 128
TOP = 8
SEQ_DEV = 16
SEQS = 512
EXPERTS = 32
CAP = 8


def draw_queries(key, part):
    shape = (SEQS, HEADS, LATENT + ROPE)
    values = jax.random.normal(jax.random.fold_in(key, 21), shape, jnp.float32)
    return values.astype(jnp.bfloat16)


def draw_latent_cache(key, part):
    shape = (SEQS, CACHE, LATENT + ROPE)
    values = jax.random.normal(jax.random.fold_in(key, 31), shape, jnp.float32)
    return values.astype(jnp.bfloat16)


def levels(rng, extent, pieces, low, top_value):
    level, own = 1.0, jax.random.fold_in(rng, 6)
    for dim, parts in pieces:
        heights = jnp.exp(jax.random.uniform(jax.random.fold_in(own, dim), (parts,), jnp.float32, low / len(pieces), top_value / len(pieces)))
        level = level * jnp.repeat(heights, extent[dim] // parts).reshape([-1 if axis == dim else 1 for axis in range(len(extent))])
    return level


def length_profile(amount, total, limit, slope):
    portions = [(1 << 20) // math.isqrt(standing ** slope) + 1 for standing in range(2, amount + 1)]
    surplus, given = total - limit - (amount - 1), [1] * (amount - 1)
    while surplus > 0:
        candidates = [i for i in range(amount - 1) if given[i] < limit]
        pool, left = sum([portions[i] for i in candidates]), surplus
        for i in candidates:
            extra = min(limit - given[i], max(1, left * portions[i] // pool), surplus)
            given[i] = given[i] + extra
            surplus = surplus - extra
    return np.array([limit] + given)


def ragged_sizes(own_key, count, total, limit, slope):
    if count == 2:
        one = jax.random.randint(own_key, (), max(1, total - limit), min(limit, total - 1) + 1)
        return jnp.stack([one, total - one])
    sizes = jnp.asarray(length_profile(count, total, limit, slope), jnp.int32)
    pairs = (count - 1) // 2
    donor, sink = sizes[1:1 + 2 * pairs:2], sizes[2:2 + 2 * pairs:2]
    margin = jnp.minimum(donor - 1, limit - sink)
    passed = jax.random.randint(jax.random.fold_in(own_key, 1), (pairs,), 0, 1 << 20) % (margin + 1)
    sizes = sizes.at[1:1 + 2 * pairs:2].set(donor - passed).at[2:2 + 2 * pairs:2].set(sink + passed)
    return sizes[jax.random.permutation(jax.random.fold_in(own_key, 2), count)]


def routed_block(stream_key, own, number, rows, number_of, top, most, lean):
    order = jax.random.permutation(stream_key, number_of)
    crowded, common = portions_of(number_of, rows * top, most, lean, True), portions_of(number_of, rows * top, most, lean, False)
    places = jnp.arange(number_of)

    def named(tallies, turn):
        used = int((tallies > 0).sum())
        fixed = max(1, used // 4)
        shifted = fixed + (places - fixed + turn * (used - fixed)) % max(1, number_of - fixed)
        return jnp.zeros((number_of,), jnp.int32).at[order[jnp.where(places < fixed, places, shifted)]].set(jnp.asarray(tallies, jnp.int32))

    tallies = jnp.where(number % 4 == 0, named(crowded, number // 4), named(common, number - number // 4 - 1))
    mixed = jax.random.permutation(jax.random.fold_in(own, 3), number_of)
    donor, taker = mixed[0:number_of // 2 * 2:2], mixed[1:number_of // 2 * 2:2]
    margin = jnp.minimum(tallies[donor] - 1, most - tallies[taker]) // 2
    margin = jnp.where((donor == order[0]) | (taker == order[0]) | (tallies[taker] == 0), 0, jnp.maximum(margin, 0))
    shifted = jax.random.randint(jax.random.fold_in(own, 4), (number_of // 2,), 0, 1 << 20) % (margin + 1)
    tallies = tallies.at[donor].add(-shifted).at[taker].add(shifted)
    items = jnp.searchsorted(jnp.cumsum(tallies), jnp.arange(rows * top), side="right").astype(jnp.int32)
    listing = items.reshape(top, rows).T
    listing = listing[jax.random.permutation(jax.random.fold_in(own, 1), rows)]
    turn = jax.random.randint(jax.random.fold_in(own, 2), (rows, 1), 0, top)
    return jnp.take_along_axis(listing, (jnp.arange(top)[None, :] + turn) % top, axis=1)


def portions_of(count, total, limit, lean, full):
    portions = [(1 << 20) // math.isqrt(grade ** lean) + 1 for grade in range(1, count + 1)]
    largest = limit if full else min(limit, max(-(-total // count), total * portions[0] // sum(portions)))
    least = 1 if total - largest >= count - 1 else 0
    holding, spare = [largest] + [least] * (count - 1), total - largest - least * (count - 1)
    while spare > 0:
        free = [i for i in range(1, count) if holding[i] < largest] or [i for i in range(1, count) if holding[i] < limit]
        pool, budget = sum([portions[i] for i in free]), spare
        for i in free:
            extra = min(limit - holding[i], max(1, budget * portions[i] // pool), spare)
            holding[i] = holding[i] + extra
            spare = spare - extra
    return np.array(holding)


def noise(stream_key, shape, scale, bound, split=(), kind=jnp.bfloat16):
    loudness = levels(stream_key, shape, split, -0.22, 0.18) if split else 1.0
    entries = jax.random.normal(stream_key, shape, jnp.float32) * scale * loudness
    return jnp.minimum(jnp.maximum(entries, -bound), bound).astype(kind)


def setup_inputs(seed: int = 0) -> dict:
    splits = jax.random.split(jax.random.key(seed), 10)
    hidden = noise(splits[0], (SEQS, D), 1.0, 6.0, ((0, 32),))
    route_ids_keys = jax.random.split(jax.random.fold_in(splits[1], 1), SEQS // SEQ_DEV)
    route_ids_turns = jax.random.permutation(jax.random.fold_in(splits[1], 3), SEQS // SEQ_DEV)
    route_ids = jax.vmap(lambda own, number: routed_block(jax.random.fold_in(splits[1], 2), own, number, SEQ_DEV, EXPERTS, TOP, CAP, 2))(route_ids_keys, route_ids_turns).reshape((SEQS, TOP))
    route_scores = jnp.clip(0.05 + 0.95 * jax.random.uniform(splits[2], (SEQS, TOP), jnp.float32) ** levels(splits[2], (SEQS, TOP), ((0, 32),), -0.2, 0.2), 0.05, 1.0)
    gate_weight = noise(splits[3], (EXPERTS, D, FF), D ** -0.5, 0.09375, ((0, 32),))
    up_weight = noise(splits[4], (EXPERTS, D, FF), D ** -0.5, 0.09375, ((0, 32),))
    down_weight = noise(splits[5], (EXPERTS, FF, D), FF ** -0.5, 0.1875, ((0, 32),))
    queries = draw_queries(jax.random.fold_in(splits[9], 71), 0)
    latent_cache = draw_latent_cache(jax.random.fold_in(splits[9], 71), 0)
    lengths = ragged_sizes(splits[8], SEQS, SEQS * CACHE // 2, CACHE, 2).astype(jnp.int32)
    return dict(hidden=hidden, route_ids=route_ids, route_scores=route_scores, gate_weight=gate_weight, up_weight=up_weight, down_weight=down_weight, queries=queries, latent_cache=latent_cache, lengths=lengths)


SOFTMAX_SCALE = 192 ** -0.5


def attention(queries, latent_cache, lengths):
    query_f = queries.astype(jnp.float32)
    cache_f = latent_cache.astype(jnp.float32)
    scores = jnp.einsum("shc,slc->shl", query_f, cache_f) * SOFTMAX_SCALE
    visible = jnp.arange(CACHE, dtype=jnp.int32)[None, None, :] < lengths[:, None, None]
    scores = jnp.where(visible, scores, jnp.float32(-1e30))
    row_max = jnp.max(scores, axis=-1, keepdims=True)
    numer = jnp.where(visible, jnp.exp(scores - row_max), jnp.float32(0.0))
    probabilities = (numer / jnp.sum(numer, axis=-1, keepdims=True)).astype(jnp.bfloat16)
    context = jnp.einsum("shl,slc->shc", probabilities.astype(jnp.float32), cache_f[:, :, :LATENT])
    return context.astype(jnp.bfloat16)


def expert_block(operands):
    buffer, w_gate, w_up, w_down = operands
    gate_part = jnp.dot(buffer, w_gate, preferred_element_type=jnp.float32)
    up_part = jnp.dot(buffer, w_up, preferred_element_type=jnp.float32)
    units = (jax.nn.silu(gate_part) * up_part).astype(jnp.bfloat16)
    return jnp.dot(units, w_down, preferred_element_type=jnp.float32).astype(jnp.bfloat16)


def reference(hidden, route_ids, route_scores, gate_weight, up_weight, down_weight, queries, latent_cache, lengths):
    combine = 2.5 * route_scores / jnp.sum(route_scores, axis=-1, keepdims=True)
    flat_ids = route_ids.reshape(-1).astype(jnp.int32)
    onehot = (flat_ids[:, None] == jnp.arange(EXPERTS, dtype=jnp.int32)[None, :]).astype(jnp.int32)
    blocks = onehot.reshape(EXPERTS, SEQ_DEV * TOP, EXPERTS)
    before = jnp.cumsum(blocks, axis=1) - blocks
    ranking = jnp.sum(before * blocks, axis=-1).reshape(-1).astype(jnp.int32)
    source = (jnp.arange(SEQS * TOP, dtype=jnp.int32) // (SEQ_DEV * TOP)).astype(jnp.int32)
    position = (source * CAP + ranking).astype(jnp.int32)
    token_of = (jnp.arange(SEQS * TOP, dtype=jnp.int32) // TOP).astype(jnp.int32)
    buffers = jnp.zeros((EXPERTS, EXPERTS * CAP, D), jnp.bfloat16).at[flat_ids, position].set(hidden[token_of])
    outputs = lax.map(expert_block, (buffers, gate_weight, up_weight, down_weight))
    picked = outputs[flat_ids, position].astype(jnp.float32).reshape(SEQS, TOP, D)
    expert_mix = jnp.sum(picked * combine[:, :, None], axis=1).astype(jnp.bfloat16)
    context = attention(queries, latent_cache, lengths)
    return (expert_mix, context)
```

```python
import functools
import heapq

import jax
import jax.numpy as jnp
from jax import lax
from jax.experimental import pallas as pl
from jax.experimental.pallas import tpu as pltpu
from jax.sharding import PartitionSpec as P

MESH = pl.DeviceIdType.MESH
LATENT = 512
SCALE = 192 ** (-0.5)
DEPTH = 4
CHUNK = 512
HOP = 4.0


def bits_of(rows, cols):
    tall = cols // DEPTH
    bits = {"z": [], "y": [], "x": []}
    for axis, size, mesh_axis, stride in (("z", DEPTH, "col", tall), ("y", tall, "col", 1), ("x", rows // 2, "row", 2)):
        step = size // 2
        while step >= 1:
            bits[axis].append((axis, mesh_axis, stride * step, step))
            step //= 2
    return bits["z"] + bits["y"] + bits["x"] + [("core", "row", 1, 1 / 6)]


def runs_of(slots):
    runs = []
    for slot in sorted(slots):
        if runs and runs[-1][0] + runs[-1][1] == slot:
            runs[-1][1] += 1
        else:
            runs.append([slot, 1])
    return [tuple(run) for run in runs]


def held_before(order, stage):
    slots = [0]
    for bit in order[:stage]:
        slots += [slot | (1 << bit) for slot in slots]
    return sorted(slots)


def schedule(bits, orders, widths, backward, lead):
    stages = len(bits)
    free, heap, out = {}, [], []
    for chunk, width in enumerate(widths):
        heapq.heappush(heap, (lead * chunk + (0.01 if width == CHUNK else 0.0), chunk, 0))
    while heap:
        ready, chunk, step = heapq.heappop(heap)
        out.append((chunk, step, ready))
        if step == stages:
            continue
        stage = stages - 1 - step if backward else step
        link = orders[chunk][stage]
        start = max(ready, free.get(link, 0.0))
        end = start + (1 << stage) * bits[link][3] * widths[chunk] / CHUNK
        free[link] = end
        heapq.heappush(heap, (end + HOP, chunk, step + 1))
    return out


def kernel(
    plan,
    ids_ref, scores_ref, len_ref, hidden_ref, wg_hbm, wu_hbm, wd_hbm, q_hbm, kv_hbm,
    mix_ref, ctx_hbm,
    xg, got, wg, wu, wd, qv, kv, ctx, pick, place, share, xc, gacc, uacc, units,
    gs_sem, gr_sem, ss_sem, sr_sem, w_sem, a_sem,
):
    bits, orders, ext, cap, rows, cols = plan
    stages, chunks = len(bits), len(orders) - 1
    seqs, width = hidden_ref.shape
    devices = rows * cols
    row, col = lax.axis_index("row"), lax.axis_index("col")
    me = row * cols + col

    def partner(bit):
        _, mesh_axis, stride, _ = bits[bit]
        own = row if mesh_axis == "row" else col
        other = own + stride * (1 - 2 * lax.rem(lax.div(own, stride), 2))
        return (other, col) if mesh_axis == "row" else (row, other)

    barrier = pltpu.get_barrier_semaphore()
    for bit in range(stages):
        pl.semaphore_signal(barrier, inc=1, device_id=partner(bit), device_id_type=MESH)

    loads = [
        pltpu.make_async_copy(q_hbm, qv, a_sem.at[0]),
        pltpu.make_async_copy(kv_hbm, kv, a_sem.at[1]),
    ]
    for load in loads:
        load.start()
    weight_loads = []
    for chunk in range(chunks):
        part = pl.ds(chunk * CHUNK, CHUNK)
        weight_loads.append((
            pltpu.make_async_copy(wg_hbm.at[0, part], wg.at[part], w_sem.at[0, chunk]),
            pltpu.make_async_copy(wu_hbm.at[0, part], wu.at[part], w_sem.at[1, chunk]),
        ))
    down_loads = [
        pltpu.make_async_copy(
            wd_hbm.at[0, :, pl.ds(chunk * CHUNK, CHUNK)], wd.at[:, pl.ds(chunk * CHUNK, CHUNK)], w_sem.at[2, chunk]
        )
        for chunk in range(chunks)
    ]

    scores = scores_ref[...]
    combine = 2.5 * scores / jnp.sum(scores, axis=-1, keepdims=True)
    ids = ids_ref[...]
    lane = lax.broadcasted_iota(jnp.int32, (seqs, ext), 1)
    table = jnp.zeros((seqs, ext), jnp.float32)
    for k in range(ids.shape[1]):
        weight = combine[:, k : k + 1]
        high = weight.astype(jnp.bfloat16).astype(jnp.float32)
        table += jnp.where(lane == ids[:, k : k + 1], high, 0.0)
        table += jnp.where(lane == ids[:, k : k + 1] + devices, weight - high, 0.0)
    xg[0, :, pl.ds(0, ext)] = table.astype(jnp.bfloat16)
    xg[0, :, pl.ds(ext, width)] = hidden_ref[...]
    pl.semaphore_wait(barrier, stages)

    def columns(chunk):
        return pl.ds(0, ext) if chunk == chunks else pl.ds(ext + chunk * CHUNK, CHUNK)

    def gather_start(chunk, stage):
        bit = orders[chunk][stage]
        for first, count in runs_of(held_before(orders[chunk], stage)):
            pltpu.make_async_remote_copy(
                src_ref=xg.at[pl.ds(first, count), :, columns(chunk)],
                dst_ref=xg.at[pl.ds(first + (1 << bit), count), :, columns(chunk)],
                send_sem=gs_sem.at[chunk, stage], recv_sem=gr_sem.at[chunk, stage],
                device_id=partner(bit), device_id_type=MESH,
            ).start()

    def gather_wait(chunk, stage, sem):
        view = xg.at[pl.ds(0, 1 << stage), :, columns(chunk)]
        pltpu.make_async_copy(view, view, sem.at[chunk, stage]).wait()

    groups = devices // 16
    tokens = 16 * seqs
    slots = 16 * cap

    def routing():
        lane_of = lax.broadcasted_iota(jnp.int32, (16, ext), 1)
        row_of = lax.broadcasted_iota(jnp.int32, (16, ext), 0)
        chosen = jnp.where(lane_of == me + row_of * devices, 1.0, 0.0)
        chosen = jnp.where(row_of < 2, chosen, 0.0).astype(jnp.bfloat16)
        before = lax.broadcasted_iota(jnp.int32, (tokens, tokens), 0)
        after = lax.broadcasted_iota(jnp.int32, (tokens, tokens), 1)
        earlier = jnp.where((before // seqs == after // seqs) & (before < after), 1.0, 0.0).astype(jnp.bfloat16)
        slot = lax.broadcasted_iota(jnp.int32, (slots, tokens), 0)
        token = lax.broadcasted_iota(jnp.int32, (slots, tokens), 1)
        for group in range(groups):
            table = xg[pl.ds(16 * group, 16), :, pl.ds(0, ext)].reshape(tokens, ext)
            both = lax.dot_general(chosen, table, (((1,), (1,)), ((), ())), preferred_element_type=jnp.float32)
            named = jnp.where(both > 0.0, 1.0, 0.0)
            rank = jnp.dot(named.astype(jnp.bfloat16), earlier, preferred_element_type=jnp.float32)[0:1].astype(jnp.int32)
            weight = both[0:1] + both[1:2]
            hit = (slot // cap == token // seqs) & (rank == slot % cap) & (named[0:1] > 0.0)
            one = jnp.where(hit, 1.0, 0.0)
            share[pl.ds(group * slots, slots), :] = jnp.broadcast_to(
                jnp.sum(one * weight, axis=1, keepdims=True), (slots, 128)
            )
            pick[group] = one.astype(jnp.bfloat16)
            place[group] = one.T.astype(jnp.bfloat16)

    tile = 256
    total = groups * slots

    def up_chunk(chunk, first):
        here = pl.ds(ext + chunk * CHUNK, CHUNK)
        for group in range(groups):
            x = xg[pl.ds(16 * group, 16), :, here].reshape(tokens, CHUNK)
            xc[pl.ds(group * slots, slots), :] = jnp.dot(
                pick[group], x, preferred_element_type=jnp.float32
            ).astype(jnp.bfloat16)
        for load in weight_loads[chunk]:
            load.wait()

        def body(n, carry):
            at = pl.ds(pl.multiple_of(n * tile, tile), tile)
            for acc, w in ((gacc, wg), (uacc, wu)):
                part = jnp.dot(xc[...], w[pl.ds(chunk * CHUNK, CHUNK), at], preferred_element_type=jnp.float32)
                acc[:, at] = part if first else acc[:, at] + part
            return carry

        lax.fori_loop(0, gacc.shape[1] // tile, body, 0)

    def down_chunk(chunk):
        down_loads[chunk].wait()

        def body(n, carry):
            at = pl.ds(pl.multiple_of(chunk * CHUNK + n * tile, tile), tile)
            to = pl.ds(pl.multiple_of(ext + chunk * CHUNK + n * tile, 128), tile)
            out = jnp.dot(units[...], wd[:, at], preferred_element_type=jnp.float32)
            out = (out * share[:, 0:1]).astype(jnp.bfloat16)
            for group in range(groups):
                y = jnp.dot(place[group], out[group * slots : (group + 1) * slots], preferred_element_type=jnp.float32)
                xg[pl.ds(16 * group, 16), :, to] = y.astype(jnp.bfloat16).reshape(16, seqs, tile)
            return carry

        lax.fori_loop(0, CHUNK // tile, body, 0)

    def attend(first, count):
        def body(i, carry):
            query, cache = qv[i], kv[i]
            scored = lax.dot_general(query, cache, (((1,), (1,)), ((), ())), preferred_element_type=jnp.float32) * SCALE
            visible = lax.broadcasted_iota(jnp.int32, scored.shape, 1) < len_ref[i]
            scored = jnp.where(visible, scored, -1e30)
            numer = jnp.where(visible, jnp.exp(scored - jnp.max(scored, axis=-1, keepdims=True)), 0.0)
            prob = (numer / jnp.sum(numer, axis=-1, keepdims=True)).astype(jnp.bfloat16)
            ctx[i] = jnp.dot(prob, cache[:, :LATENT], preferred_element_type=jnp.float32).astype(jnp.bfloat16)
            return carry

        lax.fori_loop(first, first + count, body, 0, unroll=2 if count % 2 == 0 else 1)

    widths = [CHUNK] * chunks + [ext]
    events = schedule(bits, orders, widths, False, 0.0)
    attend_from = chunks + 2
    attended = 0
    first_up = True
    started_weights = False
    for number, (chunk, step, _) in enumerate(events):
        if step > 0:
            gather_wait(chunk, step - 1, gr_sem)
        if step < stages:
            gather_start(chunk, step)
        elif chunk == chunks:
            assert first_up
            routing()
        else:
            up_chunk(chunk, first_up)
            first_up = False
        if not started_weights and number == chunks:
            started_weights = True
            for pair in weight_loads:
                for load in pair:
                    load.start()
            for load in down_loads:
                load.start()
        if number >= attend_from and attended < seqs and (number - attend_from) % 2 == 0:
            if attended == 0:
                for load in loads:
                    load.wait()
            attend(attended, 2)
            attended += 2
    if attended < seqs:
        attend(attended, seqs - attended)
    ctx_out = pltpu.make_async_copy(ctx, ctx_hbm, a_sem.at[2])
    ctx_out.start()

    def act(n, carry):
        at = pl.ds(pl.multiple_of(n * tile, tile), tile)
        gate = gacc[:, at]
        units[:, at] = (gate / (1.0 + jnp.exp(-gate)) * uacc[:, at]).astype(jnp.bfloat16)
        return carry

    lax.fori_loop(0, gacc.shape[1] // tile, act, 0)
    for chunk in range(chunks + 1):
        for stage in range(stages):
            gather_wait(chunk, stage, gs_sem)

    def scatter_start(chunk, stage):
        bit = orders[chunk][stage]
        at = 1 << stage
        for first, count in runs_of(held_before(orders[chunk], stage)):
            pltpu.make_async_remote_copy(
                src_ref=xg.at[pl.ds(first + (1 << bit), count), :, pl.ds(ext + chunk * CHUNK, CHUNK)],
                dst_ref=got.at[pl.ds(at, count), :, pl.ds(chunk * CHUNK, CHUNK)],
                send_sem=ss_sem.at[chunk, stage], recv_sem=sr_sem.at[chunk, stage],
                device_id=partner(bit), device_id_type=MESH,
            ).start()
            at += count

    def scatter_wait(chunk, stage, sem):
        view = got.at[pl.ds(1 << stage, 1 << stage), :, pl.ds(chunk * CHUNK, CHUNK)]
        pltpu.make_async_copy(view, view, sem.at[chunk, stage]).wait()

    def add(chunk, stage):
        at = 1 << stage
        here, there = pl.ds(ext + chunk * CHUNK, CHUNK), pl.ds(chunk * CHUNK, CHUNK)
        for first, count in runs_of(held_before(orders[chunk], stage)):

            def body(i, carry, first=first, at=at):
                both = xg[first + i, :, here].astype(jnp.float32) + got[at + i, :, there].astype(jnp.float32)
                xg[first + i, :, here] = both.astype(jnp.bfloat16)
                return carry

            lax.fori_loop(0, count, body, 0, unroll=min(count, 2))
            at += count

    for chunk, step, _ in schedule(bits, orders, [CHUNK] * chunks, True, 1.5):
        if step == 0:
            down_chunk(chunk)
        else:
            stage = stages - step
            scatter_wait(chunk, stage, sr_sem)
            if stage > 0:
                add(chunk, stage)
        if step < stages:
            scatter_start(chunk, stages - 1 - step)
        else:
            here, there = pl.ds(ext + chunk * CHUNK, CHUNK), pl.ds(chunk * CHUNK, CHUNK)
            both = xg[0, :, here].astype(jnp.float32) + got[1, :, there].astype(jnp.float32)
            mix_ref[:, there] = both.astype(jnp.bfloat16)
    for chunk in range(chunks):
        for stage in range(stages):
            scatter_wait(chunk, stage, ss_sem)
    ctx_out.wait()


def shards(rows, cols, hidden, route_ids, route_scores, gate_weight, up_weight, down_weight, queries, cache, lengths):
    seqs, width = hidden.shape
    hidden_units = gate_weight.shape[2]
    devices = rows * cols
    cap = max(2, 2 * seqs * route_ids.shape[1] // devices)
    ext = -(-2 * devices // 128) * 128
    bits = bits_of(rows, cols)
    stages = len(bits)
    z = [i for i, bit in enumerate(bits) if bit[0] == "z"]
    y = [i for i, bit in enumerate(bits) if bit[0] == "y"]
    x = [i for i, bit in enumerate(bits) if bit[0] == "x"]
    core = [stages - 1]
    chunks = width // CHUNK
    orders = [z + x + y, x + y + z, y + z + x, x + z + y, y + x + z, z + x + y, z + y + x]
    orders = [orders[i % len(orders)] + core for i in range(chunks)] + [z + y + x + core]
    groups = devices // 16
    slots = groups * 16 * cap
    sems = pltpu.SemaphoreType.DMA((chunks + 1, stages))
    vmem = pl.BlockSpec(memory_space=pltpu.VMEM)
    hbm = pl.BlockSpec(memory_space=pl.ANY)
    bf16, f32 = jnp.bfloat16, jnp.float32
    return pl.pallas_call(
        functools.partial(kernel, (bits, orders, ext, cap, rows, cols)),
        out_shape=(
            jax.ShapeDtypeStruct((seqs, width), bf16),
            jax.ShapeDtypeStruct(queries.shape[:2] + (LATENT,), bf16),
        ),
        in_specs=[vmem, vmem, pl.BlockSpec(memory_space=pltpu.SMEM), vmem, hbm, hbm, hbm, hbm, hbm],
        out_specs=(vmem, hbm),
        scratch_shapes=[
            pltpu.VMEM((devices, seqs, ext + width), bf16),
            pltpu.VMEM((devices, seqs, width), bf16),
            pltpu.VMEM(gate_weight.shape[1:], bf16),
            pltpu.VMEM(up_weight.shape[1:], bf16),
            pltpu.VMEM(down_weight.shape[1:], bf16),
            pltpu.VMEM(queries.shape, bf16),
            pltpu.VMEM(cache.shape, bf16),
            pltpu.VMEM(queries.shape[:2] + (LATENT,), bf16),
            pltpu.VMEM((groups, 16 * cap, 16 * seqs), bf16),
            pltpu.VMEM((groups, 16 * seqs, 16 * cap), bf16),
            pltpu.VMEM((slots, 128), f32),
            pltpu.VMEM((slots, CHUNK), bf16),
            pltpu.VMEM((slots, hidden_units), f32),
            pltpu.VMEM((slots, hidden_units), f32),
            pltpu.VMEM((slots, hidden_units), bf16),
            sems, sems, sems, sems,
            pltpu.SemaphoreType.DMA((3, chunks)),
            pltpu.SemaphoreType.DMA((3,)),
        ],
        compiler_params=pltpu.CompilerParams(
            collective_id=0, has_side_effects=True, vmem_limit_bytes=62 * 1024 * 1024
        ),
    )(route_ids, route_scores, lengths, hidden, gate_weight, up_weight, down_weight, queries, cache)


def solution(mesh):
    both = ("row", "col")
    flat, deep = P(both, None), P(both, None, None)
    return jax.shard_map(
        functools.partial(shards, mesh.shape["row"], mesh.shape["col"]),
        mesh=mesh,
        in_specs=(flat, flat, flat, deep, deep, deep, deep, deep, P(both)),
        out_specs=(flat, deep),
        check_vma=False,
    )
```

```python
import functools

import jax
import jax.numpy as jnp
from jax import lax
from jax.experimental import pallas as pl
from jax.experimental.pallas import tpu as pltpu
from jax.sharding import PartitionSpec as P

MESH = pl.DeviceIdType.MESH
LATENT = 512
SCALE = 192 ** (-0.5)
DEPTH = 4
CHUNK = 512
HOP, BLOCK, WORK, FILL, FILL_FROM = 1.0, 0.38, 0.9, 1.5, 2.0


def bits_of(rows, cols):
    tall = cols // DEPTH
    bits = {"z": [], "y": [], "x": []}
    for axis, size, mesh_axis, stride in (("z", DEPTH, "col", tall), ("y", tall, "col", 1), ("x", rows // 2, "row", 2)):
        step = size // 2
        while step >= 1:
            bits[axis].append((axis, mesh_axis, stride * step, step))
            step //= 2
    return bits["z"] + bits["y"] + bits["x"] + [("core", "row", 1, 1 / 6)]


def runs_of(slots):
    runs = []
    for slot in sorted(slots):
        if runs and runs[-1][0] + runs[-1][1] == slot:
            runs[-1][1] += 1
        else:
            runs.append([slot, 1])
    return [tuple(run) for run in runs]


def held_before(order, stage):
    slots = [0]
    for bit in order[:stage]:
        slots += [slot | (1 << bit) for slot in slots]
    return sorted(slots)


def schedule(bits, orders, widths, backward, fillers):
    stages = len(bits)
    clock, free, out = 0.0, {}, []
    hops = [] if backward else [(0.0, chunk, 0) for chunk in range(len(orders))]
    if not backward:
        hops[-1] = (-1.0, len(orders) - 1, 0)
    work = list(range(len(orders))) if backward else []
    fill = list(range(fillers))
    table = backward
    while hops or work or fill:
        hops.sort()
        due = hops[0][0] if hops else float("inf")
        if due > clock + 0.2 and ((work and table) or (fill and clock > FILL_FROM)):
            if work and table:
                chunk = work.pop(0)
                out.append(("work", chunk, 0))
                clock += WORK
                if backward:
                    hops.append((clock, chunk, 0))
            else:
                out.append(("fill", fill.pop(0), 0))
                clock += FILL
            continue
        if not hops:
            clock += 0.5
            continue
        _, chunk, step = hops.pop(0)
        clock = max(clock, due) + 0.1
        out.append(("hop", chunk, step))
        if step > 0 and backward:
            clock += 0.02 * (1 << (stages - step))
        if step == stages:
            if widths[chunk] != CHUNK:
                table = True
                clock += 1.0
            elif not backward:
                work.append(chunk)
            continue
        stage = stages - 1 - step if backward else step
        link = orders[chunk][stage]
        start = max(clock, free.get(link, 0.0))
        end = start + (1 << stage) * bits[link][3] * widths[chunk] / CHUNK * BLOCK
        free[link] = end
        hops.append((end + HOP, chunk, step + 1))
    return out, clock


def kernel(
    plan,
    ids_ref, scores_ref, len_ref, hidden_ref, wg_hbm, wu_hbm, wd_hbm, q_hbm, kv_hbm,
    mix_ref, ctx_hbm,
    xg, got, wg, wu, wd, qv, kv, ctx, pick, place, share, xc, gacc, uacc, units,
    gs_sem, gr_sem, ss_sem, sr_sem, w_sem, a_sem,
):
    bits, orders, ext, cap, rows, cols = plan
    stages, chunks = len(bits), len(orders) - 1
    seqs, width = hidden_ref.shape
    devices = rows * cols
    row, col = lax.axis_index("row"), lax.axis_index("col")
    me = row * cols + col

    def partner(bit):
        _, mesh_axis, stride, _ = bits[bit]
        own = row if mesh_axis == "row" else col
        other = own + stride * (1 - 2 * lax.rem(lax.div(own, stride), 2))
        return (other, col) if mesh_axis == "row" else (row, other)

    barrier = pltpu.get_barrier_semaphore()
    for bit in range(stages):
        pl.semaphore_signal(barrier, inc=1, device_id=partner(bit), device_id_type=MESH)

    loads = [
        pltpu.make_async_copy(q_hbm, qv, a_sem.at[0]),
        pltpu.make_async_copy(kv_hbm, kv, a_sem.at[1]),
    ]
    for load in loads:
        load.start()
    weight_loads = []
    for chunk in range(chunks):
        part = pl.ds(chunk * CHUNK, CHUNK)
        weight_loads.append((
            pltpu.make_async_copy(wg_hbm.at[0, part], wg.at[part], w_sem.at[0, chunk]),
            pltpu.make_async_copy(wu_hbm.at[0, part], wu.at[part], w_sem.at[1, chunk]),
        ))
    down_loads = [
        pltpu.make_async_copy(
            wd_hbm.at[0, :, pl.ds(chunk * CHUNK, CHUNK)], wd.at[:, pl.ds(chunk * CHUNK, CHUNK)], w_sem.at[2, chunk]
        )
        for chunk in range(chunks)
    ]

    scores = scores_ref[...]
    combine = 2.5 * scores / jnp.sum(scores, axis=0, keepdims=True)
    ids = ids_ref[...]
    square = (seqs, seqs)
    diagonal = lax.broadcasted_iota(jnp.int32, square, 0) == lax.broadcasted_iota(jnp.int32, square, 1)
    lane = lax.broadcasted_iota(jnp.int32, (seqs, ext), 1)
    table = jnp.zeros((seqs, ext), jnp.float32)
    for k in range(ids.shape[0]):
        weight = jnp.sum(jnp.where(diagonal, combine[k : k + 1], 0.0), axis=1, keepdims=True)
        expert = jnp.sum(jnp.where(diagonal, ids[k : k + 1].astype(jnp.float32), 0.0), axis=1, keepdims=True)
        expert = expert.astype(jnp.int32)
        high = weight.astype(jnp.bfloat16).astype(jnp.float32)
        table += jnp.where(lane == expert, high, 0.0) + jnp.where(lane == expert + devices, weight - high, 0.0)
    xg[0, :, pl.ds(0, ext)] = table.astype(jnp.bfloat16)
    xg[0, :, pl.ds(ext, width)] = hidden_ref[...]
    pl.semaphore_wait(barrier, stages)

    def columns(chunk):
        return pl.ds(0, ext) if chunk == chunks else pl.ds(ext + chunk * CHUNK, CHUNK)

    def gather_start(chunk, stage):
        bit = orders[chunk][stage]
        for first, count in runs_of(held_before(orders[chunk], stage)):
            pltpu.make_async_remote_copy(
                src_ref=xg.at[pl.ds(first, count), :, columns(chunk)],
                dst_ref=xg.at[pl.ds(first + (1 << bit), count), :, columns(chunk)],
                send_sem=gs_sem.at[chunk, stage], recv_sem=gr_sem.at[chunk, stage],
                device_id=partner(bit), device_id_type=MESH,
            ).start()

    def gather_wait(chunk, stage, sem):
        view = xg.at[pl.ds(0, 1 << stage), :, columns(chunk)]
        pltpu.make_async_copy(view, view, sem.at[chunk, stage]).wait()

    groups = devices // 16
    tokens = 16 * seqs
    slots = 16 * cap

    def routing():
        lane_of = lax.broadcasted_iota(jnp.int32, (16, ext), 1)
        row_of = lax.broadcasted_iota(jnp.int32, (16, ext), 0)
        chosen = jnp.where(lane_of == me + row_of * devices, 1.0, 0.0)
        chosen = jnp.where(row_of < 2, chosen, 0.0).astype(jnp.bfloat16)
        before = lax.broadcasted_iota(jnp.int32, (tokens, tokens), 0)
        after = lax.broadcasted_iota(jnp.int32, (tokens, tokens), 1)
        earlier = jnp.where((before // seqs == after // seqs) & (before < after), 1.0, 0.0).astype(jnp.bfloat16)
        slot = lax.broadcasted_iota(jnp.int32, (slots, tokens), 0)
        token = lax.broadcasted_iota(jnp.int32, (slots, tokens), 1)
        for group in range(groups):
            table = xg[pl.ds(16 * group, 16), :, pl.ds(0, ext)].reshape(tokens, ext)
            both = lax.dot_general(chosen, table, (((1,), (1,)), ((), ())), preferred_element_type=jnp.float32)
            named = jnp.where(both > 0.0, 1.0, 0.0)
            rank = jnp.dot(named.astype(jnp.bfloat16), earlier, preferred_element_type=jnp.float32)[0:1].astype(jnp.int32)
            weight = both[0:1] + both[1:2]
            hit = (slot // cap == token // seqs) & (rank == slot % cap) & (named[0:1] > 0.0)
            one = jnp.where(hit, 1.0, 0.0)
            share[pl.ds(group * slots, slots), :] = jnp.broadcast_to(
                jnp.sum(one * weight, axis=1, keepdims=True), (slots, 128)
            )
            pick[group] = one.astype(jnp.bfloat16)
            place[group] = one.T.astype(jnp.bfloat16)

    tile = 256
    total = groups * slots

    def up_chunk(chunk, first):
        here = pl.ds(ext + chunk * CHUNK, CHUNK)
        for group in range(groups):
            x = xg[pl.ds(16 * group, 16), :, here].reshape(tokens, CHUNK)
            xc[pl.ds(group * slots, slots), :] = jnp.dot(
                pick[group], x, preferred_element_type=jnp.float32
            ).astype(jnp.bfloat16)
        for load in weight_loads[chunk]:
            load.wait()

        def body(n, carry):
            at = pl.ds(pl.multiple_of(n * tile, tile), tile)
            for acc, w in ((gacc, wg), (uacc, wu)):
                part = jnp.dot(xc[...], w[pl.ds(chunk * CHUNK, CHUNK), at], preferred_element_type=jnp.float32)
                acc[:, at] = part if first else acc[:, at] + part
            return carry

        lax.fori_loop(0, gacc.shape[1] // tile, body, 0)

    def down_chunk(chunk):
        down_loads[chunk].wait()

        def body(n, carry):
            at = pl.ds(pl.multiple_of(chunk * CHUNK + n * tile, tile), tile)
            to = pl.ds(pl.multiple_of(ext + chunk * CHUNK + n * tile, 128), tile)
            out = jnp.dot(units[...], wd[:, at], preferred_element_type=jnp.float32)
            out = (out * share[:, 0:1]).astype(jnp.bfloat16)
            for group in range(groups):
                y = jnp.dot(place[group], out[group * slots : (group + 1) * slots], preferred_element_type=jnp.float32)
                xg[pl.ds(16 * group, 16), :, to] = y.astype(jnp.bfloat16).reshape(16, seqs, tile)
            return carry

        lax.fori_loop(0, CHUNK // tile, body, 0)

    group_of = min(4, seqs)

    def attend(first):
        own = range(first, first + group_of)
        scored = [jnp.dot(qv[i], kv[i], preferred_element_type=jnp.float32) * SCALE for i in own]
        slot = lax.broadcasted_iota(jnp.int32, scored[0].shape, 1)
        visible = [slot < len_ref[i] for i in own]
        scored = [jnp.where(seen, each, -1e30) for seen, each in zip(visible, scored)]
        top = [jnp.max(each, axis=-1, keepdims=True) for each in scored]
        numer = [jnp.where(seen, jnp.exp(each - most), 0.0) for seen, each, most in zip(visible, scored, top)]
        total = [jnp.sum(each, axis=-1, keepdims=True) for each in numer]
        prob = [(each / whole).astype(jnp.bfloat16) for each, whole in zip(numer, total)]
        for i, each in zip(own, prob):
            ctx[i] = lax.dot_general(
                each, kv[i, pl.ds(0, LATENT), :], (((1,), (1,)), ((), ())), preferred_element_type=jnp.float32
            ).astype(jnp.bfloat16)

    widths = [CHUNK] * chunks + [ext]
    steps, _ = schedule(bits, orders, widths, False, seqs // group_of)
    first_up = True
    for number, (kind, which, step) in enumerate(steps):
        if kind == "hop":
            if step > 0:
                gather_wait(which, step - 1, gr_sem)
            if step < stages:
                gather_start(which, step)
            elif which == chunks:
                routing()
        elif kind == "work":
            up_chunk(which, first_up)
            first_up = False
        else:
            if which == 0:
                for load in loads:
                    load.wait()
            attend(which * group_of)
        if number == chunks:
            for pair in weight_loads:
                for load in pair:
                    load.start()
            for load in down_loads:
                load.start()
    ctx_out = pltpu.make_async_copy(ctx, ctx_hbm, a_sem.at[2])
    ctx_out.start()

    def act(n, carry):
        at = pl.ds(pl.multiple_of(n * tile, tile), tile)
        gate = gacc[:, at]
        units[:, at] = (gate / (1.0 + jnp.exp(-gate)) * uacc[:, at]).astype(jnp.bfloat16)
        return carry

    lax.fori_loop(0, gacc.shape[1] // tile, act, 0)
    for chunk in range(chunks + 1):
        for stage in range(stages):
            gather_wait(chunk, stage, gs_sem)

    def scatter_start(chunk, stage):
        bit = orders[chunk][stage]
        at = 1 << stage
        for first, count in runs_of(held_before(orders[chunk], stage)):
            pltpu.make_async_remote_copy(
                src_ref=xg.at[pl.ds(first + (1 << bit), count), :, pl.ds(ext + chunk * CHUNK, CHUNK)],
                dst_ref=got.at[pl.ds(at, count), :, pl.ds(chunk * CHUNK, CHUNK)],
                send_sem=ss_sem.at[chunk, stage], recv_sem=sr_sem.at[chunk, stage],
                device_id=partner(bit), device_id_type=MESH,
            ).start()
            at += count

    def scatter_wait(chunk, stage, sem):
        view = got.at[pl.ds(1 << stage, 1 << stage), :, pl.ds(chunk * CHUNK, CHUNK)]
        pltpu.make_async_copy(view, view, sem.at[chunk, stage]).wait()

    def add(chunk, stage):
        at = 1 << stage
        here, there = pl.ds(ext + chunk * CHUNK, CHUNK), pl.ds(chunk * CHUNK, CHUNK)
        def one(slot, place):
            both = xg[slot, :, here].astype(jnp.float32) + got[place, :, there].astype(jnp.float32)
            xg[slot, :, here] = both.astype(jnp.bfloat16)

        for first, count in runs_of(held_before(orders[chunk], stage)):
            if count <= 4:
                for i in range(count):
                    one(first + i, at + i)
            else:

                def body(n, carry, first=first, at=at):
                    for i in range(4):
                        one(first + 4 * n + i, at + 4 * n + i)
                    return carry

                lax.fori_loop(0, count // 4, body, 0)
            at += count

    steps, _ = schedule(bits, orders[:chunks], [CHUNK] * chunks, True, 0)
    for kind, chunk, step in steps:
        if kind == "work":
            down_chunk(chunk)
            continue
        if step > 0:
            stage = stages - step
            scatter_wait(chunk, stage, sr_sem)
            if stage > 0:
                add(chunk, stage)
        if step < stages:
            scatter_start(chunk, stages - 1 - step)
        else:
            here, there = pl.ds(ext + chunk * CHUNK, CHUNK), pl.ds(chunk * CHUNK, CHUNK)
            both = xg[0, :, here].astype(jnp.float32) + got[1, :, there].astype(jnp.float32)
            mix_ref[:, there] = both.astype(jnp.bfloat16)
    for chunk in range(chunks):
        for stage in range(stages):
            scatter_wait(chunk, stage, ss_sem)
    ctx_out.wait()


def shards(rows, cols, hidden, route_ids, route_scores, gate_weight, up_weight, down_weight, queries, cache, lengths):
    seqs, width = hidden.shape
    hidden_units = gate_weight.shape[2]
    devices = rows * cols
    cap = max(2, 2 * seqs * route_ids.shape[1] // devices)
    ext = -(-2 * devices // 128) * 128
    bits = bits_of(rows, cols)
    stages = len(bits)
    z = [i for i, bit in enumerate(bits) if bit[0] == "z"]
    y = [i for i, bit in enumerate(bits) if bit[0] == "y"]
    x = [i for i, bit in enumerate(bits) if bit[0] == "x"]
    core = [stages - 1]
    chunks = width // CHUNK
    orders = [x + y + z, y + x + z, x + z + y, z + y + x, y + x + z, z + x + y, z + y + x]
    orders = [orders[i % len(orders)] + core for i in range(chunks)] + [z + y + x + core]
    groups = devices // 16
    slots = groups * 16 * cap
    sems = pltpu.SemaphoreType.DMA((chunks + 1, stages))
    vmem = pl.BlockSpec(memory_space=pltpu.VMEM)
    hbm = pl.BlockSpec(memory_space=pl.ANY)
    bf16, f32 = jnp.bfloat16, jnp.float32
    return pl.pallas_call(
        functools.partial(kernel, (bits, orders, ext, cap, rows, cols)),
        out_shape=(
            jax.ShapeDtypeStruct((seqs, width), bf16),
            jax.ShapeDtypeStruct(queries.shape[:2] + (LATENT,), bf16),
        ),
        in_specs=[vmem, vmem, pl.BlockSpec(memory_space=pltpu.SMEM), vmem, hbm, hbm, hbm, hbm, hbm],
        out_specs=(vmem, hbm),
        scratch_shapes=[
            pltpu.VMEM((devices, seqs, ext + width), bf16),
            pltpu.VMEM((devices, seqs, width), bf16),
            pltpu.VMEM(gate_weight.shape[1:], bf16),
            pltpu.VMEM(up_weight.shape[1:], bf16),
            pltpu.VMEM(down_weight.shape[1:], bf16),
            pltpu.VMEM(queries.shape, bf16),
            pltpu.VMEM(cache.shape[:1] + cache.shape[:0:-1], bf16),
            pltpu.VMEM(queries.shape[:2] + (LATENT,), bf16),
            pltpu.VMEM((groups, 16 * cap, 16 * seqs), bf16),
            pltpu.VMEM((groups, 16 * seqs, 16 * cap), bf16),
            pltpu.VMEM((slots, 128), f32),
            pltpu.VMEM((slots, CHUNK), bf16),
            pltpu.VMEM((slots, hidden_units), f32),
            pltpu.VMEM((slots, hidden_units), f32),
            pltpu.VMEM((slots, hidden_units), bf16),
            sems, sems, sems, sems,
            pltpu.SemaphoreType.DMA((3, chunks)),
            pltpu.SemaphoreType.DMA((3,)),
        ],
        compiler_params=pltpu.CompilerParams(
            collective_id=0, has_side_effects=True, vmem_limit_bytes=62 * 1024 * 1024
        ),
    )(
        route_ids.T, route_scores.T, lengths, hidden, gate_weight, up_weight, down_weight, queries, jnp.swapaxes(cache, 1, 2)
    )


def solution(mesh):
    both = ("row", "col")
    flat, deep = P(both, None), P(both, None, None)
    return jax.shard_map(
        functools.partial(shards, mesh.shape["row"], mesh.shape["col"]),
        mesh=mesh,
        in_specs=(flat, flat, flat, deep, deep, deep, deep, deep, P(both)),
        out_specs=(flat, deep),
        check_vma=False,
    )
```

```python
import functools

import jax
import jax.numpy as jnp
from jax import lax
from jax.experimental import pallas as pl
from jax.experimental.pallas import tpu as pltpu
from jax.sharding import PartitionSpec as P

MESH = pl.DeviceIdType.MESH
LATENT = 512
SCALE = 192 ** (-0.5)
DEPTH = 4
CHUNK = 512
HOP, BLOCK, WORK, FILL, FILL_FROM = 1.0, 0.42, 0.9, 1.5, 2.0


def bits_of(rows, cols):
    tall = cols // DEPTH
    bits = {"z": [], "y": [], "x": []}
    for axis, size, mesh_axis, stride in (("z", DEPTH, "col", tall), ("y", tall, "col", 1), ("x", rows // 2, "row", 2)):
        step = size // 2
        while step >= 1:
            bits[axis].append((axis, mesh_axis, stride * step, step))
            step //= 2
    return bits["z"] + bits["y"] + bits["x"] + [("core", "row", 1, 1 / 6)]


def runs_of(slots):
    runs = []
    for slot in sorted(slots):
        if runs and runs[-1][0] + runs[-1][1] == slot:
            runs[-1][1] += 1
        else:
            runs.append([slot, 1])
    return [tuple(run) for run in runs]


def held_before(order, stage):
    slots = [0]
    for bit in order[:stage]:
        slots += [slot | (1 << bit) for slot in slots]
    return sorted(slots)


def schedule(bits, orders, widths, backward, fillers):
    stages = len(bits)
    clock, free, out = 0.0, {}, []
    hops = [] if backward else [(0.0, chunk, 0) for chunk in range(len(orders))]
    if not backward:
        hops[-1] = (-1.0, len(orders) - 1, 0)
    work = list(range(len(orders))) if backward else []
    fill = list(range(fillers))
    table = backward
    while hops or work or fill:
        hops.sort()
        due = hops[0][0] if hops else float("inf")
        if due > clock + 0.2 and ((work and table) or (fill and clock > FILL_FROM)):
            if work and table:
                chunk = work.pop(0)
                out.append(("work", chunk, 0))
                clock += WORK
                if backward:
                    hops.append((clock, chunk, 0))
            else:
                out.append(("fill", fill.pop(0), 0))
                clock += FILL
            continue
        if not hops:
            clock += 0.5
            continue
        _, chunk, step = hops.pop(0)
        clock = max(clock, due) + 0.1
        out.append(("hop", chunk, step))
        if step > 0 and backward:
            clock += 0.02 * (1 << (stages - step))
        if step == stages:
            if widths[chunk] != CHUNK:
                table = True
                clock += 1.0
            elif not backward:
                work.append(chunk)
            continue
        stage = stages - 1 - step if backward else step
        link = orders[chunk][stage]
        axis, distance = bits[link][0], bits[link][3]
        start = max(clock, free.get(axis, 0.0))
        load = (1 << stage) * widths[chunk] / CHUNK * BLOCK
        end = start + load * distance
        free[axis] = start + load * min(distance, 1)
        hops.append((end + HOP, chunk, step + 1))
    return out, clock


def kernel(
    plan,
    ids_ref, scores_ref, len_ref, hidden_ref, wg_hbm, wu_hbm, wd_hbm, q_hbm, kv_hbm,
    mix_ref, ctx_hbm,
    xg, got, wg, wu, wd, qv, kv, ctx, pick, place, share, xc, gacc, uacc, units,
    gs_sem, gr_sem, ss_sem, sr_sem, w_sem, a_sem,
):
    bits, orders, ext, cap, rows, cols = plan
    stages, chunks = len(bits), len(orders) - 1
    seqs, width = hidden_ref.shape
    devices = rows * cols
    row, col = lax.axis_index("row"), lax.axis_index("col")
    me = row * cols + col

    def partner(bit):
        _, mesh_axis, stride, _ = bits[bit]
        own = row if mesh_axis == "row" else col
        other = own + stride * (1 - 2 * lax.rem(lax.div(own, stride), 2))
        return (other, col) if mesh_axis == "row" else (row, other)

    barrier = pltpu.get_barrier_semaphore()
    for bit in range(stages):
        pl.semaphore_signal(barrier, inc=1, device_id=partner(bit), device_id_type=MESH)

    loads = [
        pltpu.make_async_copy(q_hbm, qv, a_sem.at[0]),
        pltpu.make_async_copy(kv_hbm, kv, a_sem.at[1]),
    ]
    for load in loads:
        load.start()
    weight_loads = []
    for chunk in range(chunks):
        part = pl.ds(chunk * CHUNK, CHUNK)
        weight_loads.append((
            pltpu.make_async_copy(wg_hbm.at[0, part], wg.at[part], w_sem.at[0, chunk]),
            pltpu.make_async_copy(wu_hbm.at[0, part], wu.at[part], w_sem.at[1, chunk]),
        ))
    down_loads = [
        pltpu.make_async_copy(
            wd_hbm.at[0, :, pl.ds(chunk * CHUNK, CHUNK)], wd.at[:, pl.ds(chunk * CHUNK, CHUNK)], w_sem.at[2, chunk]
        )
        for chunk in range(chunks)
    ]

    scores = scores_ref[...]
    combine = 2.5 * scores / jnp.sum(scores, axis=0, keepdims=True)
    ids = ids_ref[...]
    square = (seqs, seqs)
    diagonal = lax.broadcasted_iota(jnp.int32, square, 0) == lax.broadcasted_iota(jnp.int32, square, 1)
    lane = lax.broadcasted_iota(jnp.int32, (seqs, ext), 1)
    table = jnp.zeros((seqs, ext), jnp.float32)
    for k in range(ids.shape[0]):
        weight = jnp.sum(jnp.where(diagonal, combine[k : k + 1], 0.0), axis=1, keepdims=True)
        expert = jnp.sum(jnp.where(diagonal, ids[k : k + 1].astype(jnp.float32), 0.0), axis=1, keepdims=True)
        expert = expert.astype(jnp.int32)
        high = weight.astype(jnp.bfloat16).astype(jnp.float32)
        table += jnp.where(lane == expert, high, 0.0) + jnp.where(lane == expert + devices, weight - high, 0.0)
    xg[0, :, pl.ds(0, ext)] = table.astype(jnp.bfloat16)
    xg[0, :, pl.ds(ext, width)] = hidden_ref[...]
    pl.semaphore_wait(barrier, stages)

    def columns(chunk):
        return pl.ds(0, ext) if chunk == chunks else pl.ds(ext + chunk * CHUNK, CHUNK)

    def gather_start(chunk, stage):
        bit = orders[chunk][stage]
        for first, count in runs_of(held_before(orders[chunk], stage)):
            pltpu.make_async_remote_copy(
                src_ref=xg.at[pl.ds(first, count), :, columns(chunk)],
                dst_ref=xg.at[pl.ds(first + (1 << bit), count), :, columns(chunk)],
                send_sem=gs_sem.at[chunk, stage], recv_sem=gr_sem.at[chunk, stage],
                device_id=partner(bit), device_id_type=MESH,
            ).start()

    def gather_wait(chunk, stage, sem):
        view = xg.at[pl.ds(0, 1 << stage), :, columns(chunk)]
        pltpu.make_async_copy(view, view, sem.at[chunk, stage]).wait()

    groups = devices // 16
    tokens = 16 * seqs
    slots = 16 * cap

    def routing():
        lane_of = lax.broadcasted_iota(jnp.int32, (16, ext), 1)
        row_of = lax.broadcasted_iota(jnp.int32, (16, ext), 0)
        chosen = jnp.where(lane_of == me + row_of * devices, 1.0, 0.0)
        chosen = jnp.where(row_of < 2, chosen, 0.0).astype(jnp.bfloat16)
        before = lax.broadcasted_iota(jnp.int32, (tokens, tokens), 0)
        after = lax.broadcasted_iota(jnp.int32, (tokens, tokens), 1)
        earlier = jnp.where((before // seqs == after // seqs) & (before < after), 1.0, 0.0).astype(jnp.bfloat16)
        slot = lax.broadcasted_iota(jnp.int32, (slots, tokens), 0)
        token = lax.broadcasted_iota(jnp.int32, (slots, tokens), 1)
        for group in range(groups):
            table = xg[pl.ds(16 * group, 16), :, pl.ds(0, ext)].reshape(tokens, ext)
            both = lax.dot_general(chosen, table, (((1,), (1,)), ((), ())), preferred_element_type=jnp.float32)
            named = jnp.where(both > 0.0, 1.0, 0.0)
            rank = jnp.dot(named.astype(jnp.bfloat16), earlier, preferred_element_type=jnp.float32)[0:1].astype(jnp.int32)
            weight = both[0:1] + both[1:2]
            hit = (slot // cap == token // seqs) & (rank == slot % cap) & (named[0:1] > 0.0)
            one = jnp.where(hit, 1.0, 0.0)
            share[pl.ds(group * slots, slots), :] = jnp.broadcast_to(
                jnp.sum(one * weight, axis=1, keepdims=True), (slots, 128)
            )
            pick[group] = one.astype(jnp.bfloat16)
            place[group] = one.T.astype(jnp.bfloat16)

    tile = 256
    total = groups * slots

    def up_chunk(chunk, first):
        here = pl.ds(ext + chunk * CHUNK, CHUNK)
        for group in range(groups):
            x = xg[pl.ds(16 * group, 16), :, here].reshape(tokens, CHUNK)
            xc[pl.ds(group * slots, slots), :] = jnp.dot(
                pick[group], x, preferred_element_type=jnp.float32
            ).astype(jnp.bfloat16)
        for load in weight_loads[chunk]:
            load.wait()

        def body(n, carry):
            at = pl.ds(pl.multiple_of(n * tile, tile), tile)
            for acc, w in ((gacc, wg), (uacc, wu)):
                part = jnp.dot(xc[...], w[pl.ds(chunk * CHUNK, CHUNK), at], preferred_element_type=jnp.float32)
                acc[:, at] = part if first else acc[:, at] + part
            return carry

        lax.fori_loop(0, gacc.shape[1] // tile, body, 0)

    def down_chunk(chunk):
        down_loads[chunk].wait()

        def body(n, carry):
            at = pl.ds(pl.multiple_of(chunk * CHUNK + n * tile, tile), tile)
            to = pl.ds(pl.multiple_of(ext + chunk * CHUNK + n * tile, 128), tile)
            out = jnp.dot(units[...], wd[:, at], preferred_element_type=jnp.float32)
            out = (out * share[:, 0:1]).astype(jnp.bfloat16)
            for group in range(groups):
                y = jnp.dot(place[group], out[group * slots : (group + 1) * slots], preferred_element_type=jnp.float32)
                xg[pl.ds(16 * group, 16), :, to] = y.astype(jnp.bfloat16).reshape(16, seqs, tile)
            return carry

        lax.fori_loop(0, CHUNK // tile, body, 0)

    group_of = min(4, seqs)

    def attend(first):
        own = range(first, first + group_of)
        scored = [jnp.dot(qv[i], kv[i], preferred_element_type=jnp.float32) * SCALE for i in own]
        slot = lax.broadcasted_iota(jnp.int32, scored[0].shape, 1)
        visible = [slot < len_ref[i] for i in own]
        scored = [jnp.where(seen, each, -1e30) for seen, each in zip(visible, scored)]
        top = [jnp.max(each, axis=-1, keepdims=True) for each in scored]
        numer = [jnp.where(seen, jnp.exp(each - most), 0.0) for seen, each, most in zip(visible, scored, top)]
        total = [jnp.sum(each, axis=-1, keepdims=True) for each in numer]
        prob = [(each / whole).astype(jnp.bfloat16) for each, whole in zip(numer, total)]
        for i, each in zip(own, prob):
            ctx[i] = lax.dot_general(
                each, kv[i, pl.ds(0, LATENT), :], (((1,), (1,)), ((), ())), preferred_element_type=jnp.float32
            ).astype(jnp.bfloat16)

    widths = [CHUNK] * chunks + [ext]
    steps, _ = schedule(bits, orders, widths, False, seqs // group_of)
    first_up = True
    for number, (kind, which, step) in enumerate(steps):
        if kind == "hop":
            if step > 0:
                gather_wait(which, step - 1, gr_sem)
            if step < stages:
                gather_start(which, step)
            elif which == chunks:
                routing()
        elif kind == "work":
            up_chunk(which, first_up)
            first_up = False
        else:
            if which == 0:
                for load in loads:
                    load.wait()
            attend(which * group_of)
        if number == chunks:
            for pair in weight_loads:
                for load in pair:
                    load.start()
            for load in down_loads:
                load.start()
    ctx_out = pltpu.make_async_copy(ctx, ctx_hbm, a_sem.at[2])
    ctx_out.start()

    def act(n, carry):
        at = pl.ds(pl.multiple_of(n * tile, tile), tile)
        gate = gacc[:, at]
        units[:, at] = (gate / (1.0 + jnp.exp(-gate)) * uacc[:, at]).astype(jnp.bfloat16)
        return carry

    lax.fori_loop(0, gacc.shape[1] // tile, act, 0)
    for chunk in range(chunks + 1):
        for stage in range(stages):
            gather_wait(chunk, stage, gs_sem)

    def scatter_start(chunk, stage):
        bit = orders[chunk][stage]
        at = 1 << stage
        for first, count in runs_of(held_before(orders[chunk], stage)):
            pltpu.make_async_remote_copy(
                src_ref=xg.at[pl.ds(first + (1 << bit), count), :, pl.ds(ext + chunk * CHUNK, CHUNK)],
                dst_ref=got.at[pl.ds(at, count), :, pl.ds(chunk * CHUNK, CHUNK)],
                send_sem=ss_sem.at[chunk, stage], recv_sem=sr_sem.at[chunk, stage],
                device_id=partner(bit), device_id_type=MESH,
            ).start()
            at += count

    def scatter_wait(chunk, stage, sem):
        view = got.at[pl.ds(1 << stage, 1 << stage), :, pl.ds(chunk * CHUNK, CHUNK)]
        pltpu.make_async_copy(view, view, sem.at[chunk, stage]).wait()

    def add(chunk, stage):
        at = 1 << stage
        here, there = pl.ds(ext + chunk * CHUNK, CHUNK), pl.ds(chunk * CHUNK, CHUNK)
        def one(slot, place):
            both = xg[slot, :, here].astype(jnp.float32) + got[place, :, there].astype(jnp.float32)
            xg[slot, :, here] = both.astype(jnp.bfloat16)

        for first, count in runs_of(held_before(orders[chunk], stage)):
            if count <= 4:
                for i in range(count):
                    one(first + i, at + i)
            else:

                def body(n, carry, first=first, at=at):
                    for i in range(4):
                        one(first + 4 * n + i, at + 4 * n + i)
                    return carry

                lax.fori_loop(0, count // 4, body, 0)
            at += count

    steps, _ = schedule(bits, orders[:chunks], [CHUNK] * chunks, True, 0)
    for kind, chunk, step in steps:
        if kind == "work":
            down_chunk(chunk)
            continue
        if step > 0:
            stage = stages - step
            scatter_wait(chunk, stage, sr_sem)
            if stage > 0:
                add(chunk, stage)
        if step < stages:
            scatter_start(chunk, stages - 1 - step)
        else:
            here, there = pl.ds(ext + chunk * CHUNK, CHUNK), pl.ds(chunk * CHUNK, CHUNK)
            both = xg[0, :, here].astype(jnp.float32) + got[1, :, there].astype(jnp.float32)
            mix_ref[:, there] = both.astype(jnp.bfloat16)
    for chunk in range(chunks):
        for stage in range(stages):
            scatter_wait(chunk, stage, ss_sem)
    ctx_out.wait()


def shards(rows, cols, hidden, route_ids, route_scores, gate_weight, up_weight, down_weight, queries, cache, lengths):
    seqs, width = hidden.shape
    hidden_units = gate_weight.shape[2]
    devices = rows * cols
    cap = max(2, 2 * seqs * route_ids.shape[1] // devices)
    ext = -(-2 * devices // 128) * 128
    bits = bits_of(rows, cols)
    stages = len(bits)
    z = [i for i, bit in enumerate(bits) if bit[0] == "z"]
    y = [i for i, bit in enumerate(bits) if bit[0] == "y"]
    x = [i for i, bit in enumerate(bits) if bit[0] == "x"]
    core = [stages - 1]
    chunks = width // CHUNK
    orders = [z + x + y, y + x + z, z + y + x, z + x + y, x + y + z, z + y + x, z + x + y]
    orders = [orders[i % len(orders)] + core for i in range(chunks)] + [z + y + x + core]
    groups = devices // 16
    slots = groups * 16 * cap
    sems = pltpu.SemaphoreType.DMA((chunks + 1, stages))
    vmem = pl.BlockSpec(memory_space=pltpu.VMEM)
    hbm = pl.BlockSpec(memory_space=pl.ANY)
    bf16, f32 = jnp.bfloat16, jnp.float32
    return pl.pallas_call(
        functools.partial(kernel, (bits, orders, ext, cap, rows, cols)),
        out_shape=(
            jax.ShapeDtypeStruct((seqs, width), bf16),
            jax.ShapeDtypeStruct(queries.shape[:2] + (LATENT,), bf16),
        ),
        in_specs=[vmem, vmem, pl.BlockSpec(memory_space=pltpu.SMEM), vmem, hbm, hbm, hbm, hbm, hbm],
        out_specs=(vmem, hbm),
        scratch_shapes=[
            pltpu.VMEM((devices, seqs, ext + width), bf16),
            pltpu.VMEM((devices, seqs, width), bf16),
            pltpu.VMEM(gate_weight.shape[1:], bf16),
            pltpu.VMEM(up_weight.shape[1:], bf16),
            pltpu.VMEM(down_weight.shape[1:], bf16),
            pltpu.VMEM(queries.shape, bf16),
            pltpu.VMEM(cache.shape[:1] + cache.shape[:0:-1], bf16),
            pltpu.VMEM(queries.shape[:2] + (LATENT,), bf16),
            pltpu.VMEM((groups, 16 * cap, 16 * seqs), bf16),
            pltpu.VMEM((groups, 16 * seqs, 16 * cap), bf16),
            pltpu.VMEM((slots, 128), f32),
            pltpu.VMEM((slots, CHUNK), bf16),
            pltpu.VMEM((slots, hidden_units), f32),
            pltpu.VMEM((slots, hidden_units), f32),
            pltpu.VMEM((slots, hidden_units), bf16),
            sems, sems, sems, sems,
            pltpu.SemaphoreType.DMA((3, chunks)),
            pltpu.SemaphoreType.DMA((3,)),
        ],
        compiler_params=pltpu.CompilerParams(
            collective_id=0, has_side_effects=True, vmem_limit_bytes=62 * 1024 * 1024
        ),
    )(
        route_ids.T, route_scores.T, lengths, hidden, gate_weight, up_weight, down_weight, queries, jnp.swapaxes(cache, 1, 2)
    )


def solution(mesh):
    both = ("row", "col")
    flat, deep = P(both, None), P(both, None, None)
    return jax.shard_map(
        functools.partial(shards, mesh.shape["row"], mesh.shape["col"]),
        mesh=mesh,
        in_specs=(flat, flat, flat, deep, deep, deep, deep, deep, P(both)),
        out_specs=(flat, deep),
        check_vma=False,
    )
```

```python
import functools

import jax
import jax.numpy as jnp
from jax import lax
from jax.experimental import pallas as pl
from jax.experimental.pallas import tpu as pltpu
from jax.sharding import PartitionSpec as P

MESH = pl.DeviceIdType.MESH
LATENT = 512
SCALE = 192 ** (-0.5)
DEPTH = 4
CHUNK = 512
HOP, BLOCK, WORK, FILL, FILL_FROM = 1.0, 0.42, 0.9, 1.5, 2.0


def bits_of(rows, cols):
    tall = cols // DEPTH
    bits = {"z": [], "y": [], "x": []}
    for axis, size, mesh_axis, stride in (("z", DEPTH, "col", tall), ("y", tall, "col", 1), ("x", rows // 2, "row", 2)):
        step = size // 2
        while step >= 1:
            bits[axis].append((axis, mesh_axis, stride * step, step))
            step //= 2
    return bits["z"] + bits["y"] + bits["x"] + [("core", "row", 1, 1 / 6)]


def runs_of(slots):
    runs = []
    for slot in sorted(slots):
        if runs and runs[-1][0] + runs[-1][1] == slot:
            runs[-1][1] += 1
        else:
            runs.append([slot, 1])
    return [tuple(run) for run in runs]


def held_before(order, stage):
    slots = [0]
    for bit in order[:stage]:
        slots += [slot | (1 << bit) for slot in slots]
    return sorted(slots)


def schedule(bits, orders, widths, backward, fillers):
    stages = len(bits)
    clock, free, out = 0.0, {}, []
    hops = [] if backward else [(0.0, chunk, 0) for chunk in range(len(orders))]
    if not backward:
        hops[-1] = (-1.0, len(orders) - 1, 0)
    work = list(range(len(orders))) if backward else []
    fill = list(range(fillers))
    table = backward
    while hops or work or fill:
        hops.sort()
        due = hops[0][0] if hops else float("inf")
        if due > clock + 0.2 and ((work and table) or (fill and clock > FILL_FROM)):
            if work and table:
                chunk = work.pop(0)
                out.append(("work", chunk, 0))
                clock += WORK
                if backward:
                    hops.append((clock, chunk, 0))
            else:
                out.append(("fill", fill.pop(0), 0))
                clock += FILL
            continue
        if not hops:
            clock += 0.5
            continue
        _, chunk, step = hops.pop(0)
        clock = max(clock, due) + 0.1
        out.append(("hop", chunk, step))
        if step > 0 and backward:
            clock += 0.02 * (1 << (stages - step))
        if step == stages:
            if widths[chunk] != CHUNK:
                table = True
                clock += 1.0
            elif not backward:
                work.append(chunk)
            continue
        stage = stages - 1 - step if backward else step
        link = orders[chunk][stage]
        axis, distance = bits[link][0], bits[link][3]
        start = max(clock, free.get(axis, 0.0))
        load = (1 << stage) * widths[chunk] / CHUNK * BLOCK
        end = start + load * distance
        free[axis] = start + load * min(distance, 1)
        hops.append((end + HOP, chunk, step + 1))
    return out, clock


def kernel(
    plan,
    ids_ref, scores_ref, len_ref, hidden_ref, wg_hbm, wu_hbm, wd_hbm, q_hbm, kv_hbm,
    mix_ref, ctx_hbm,
    xg, got, wg, wu, wd, qv, kv, ctx, pick, place, share, xc, gacc, uacc, units,
    gs_sem, gr_sem, ss_sem, sr_sem, w_sem, a_sem,
):
    bits, orders, ext, cap, rows, cols = plan
    stages, chunks = len(bits), len(orders) - 1
    seqs, width = hidden_ref.shape
    devices = rows * cols
    row, col = lax.axis_index("row"), lax.axis_index("col")
    me = row * cols + col

    def partner(bit):
        _, mesh_axis, stride, _ = bits[bit]
        own = row if mesh_axis == "row" else col
        other = own + stride * (1 - 2 * lax.rem(lax.div(own, stride), 2))
        return (other, col) if mesh_axis == "row" else (row, other)

    barrier = pltpu.get_barrier_semaphore()
    for bit in range(stages):
        pl.semaphore_signal(barrier, inc=1, device_id=partner(bit), device_id_type=MESH)

    loads = [
        pltpu.make_async_copy(q_hbm, qv, a_sem.at[0]),
        pltpu.make_async_copy(kv_hbm, kv, a_sem.at[1]),
    ]
    for load in loads:
        load.start()
    weight_loads = []
    for chunk in range(chunks):
        part = pl.ds(chunk * CHUNK, CHUNK)
        weight_loads.append((
            pltpu.make_async_copy(wg_hbm.at[0, part], wg.at[part], w_sem.at[0, chunk]),
            pltpu.make_async_copy(wu_hbm.at[0, part], wu.at[part], w_sem.at[1, chunk]),
        ))
    down_loads = [
        pltpu.make_async_copy(
            wd_hbm.at[0, :, pl.ds(chunk * CHUNK, CHUNK)], wd.at[:, pl.ds(chunk * CHUNK, CHUNK)], w_sem.at[2, chunk]
        )
        for chunk in range(chunks)
    ]

    scores = scores_ref[...]
    combine = 2.5 * scores / jnp.sum(scores, axis=0, keepdims=True)
    ids = ids_ref[...]
    square = (seqs, seqs)
    diagonal = lax.broadcasted_iota(jnp.int32, square, 0) == lax.broadcasted_iota(jnp.int32, square, 1)
    lane = lax.broadcasted_iota(jnp.int32, (seqs, ext), 1)
    table = jnp.zeros((seqs, ext), jnp.float32)
    for k in range(ids.shape[0]):
        weight = jnp.sum(jnp.where(diagonal, combine[k : k + 1], 0.0), axis=1, keepdims=True)
        expert = jnp.sum(jnp.where(diagonal, ids[k : k + 1].astype(jnp.float32), 0.0), axis=1, keepdims=True)
        expert = expert.astype(jnp.int32)
        high = weight.astype(jnp.bfloat16).astype(jnp.float32)
        table += jnp.where(lane == expert, high, 0.0) + jnp.where(lane == expert + devices, weight - high, 0.0)
    xg[0, :, pl.ds(0, ext)] = table.astype(jnp.bfloat16)
    xg[0, :, pl.ds(ext, width)] = hidden_ref[...]
    pl.semaphore_wait(barrier, stages)

    def columns(chunk):
        return pl.ds(0, ext) if chunk == chunks else pl.ds(ext + chunk * CHUNK, CHUNK)

    def gather_start(chunk, stage):
        order = orders[chunk]
        held = held_before(order, stage)
        fresh = sorted(set(held) - set(held_before(order, stage - 1))) if stage else held
        hops = [(stage, held)] if stage < stages - 1 else []
        for to, sent in hops + [(stages - 1, fresh)]:
            for first, count in runs_of(sent):
                pltpu.make_async_remote_copy(
                    src_ref=xg.at[pl.ds(first, count), :, columns(chunk)],
                    dst_ref=xg.at[pl.ds(first + (1 << order[to]), count), :, columns(chunk)],
                    send_sem=gs_sem.at[chunk, to], recv_sem=gr_sem.at[chunk, to],
                    device_id=partner(order[to]), device_id_type=MESH,
                ).start()

    def gather_wait(chunk, stage, sem):
        view = xg.at[pl.ds(0, 1 << stage), :, columns(chunk)]
        pltpu.make_async_copy(view, view, sem.at[chunk, stage]).wait()

    groups = devices // 16
    tokens = 16 * seqs
    slots = 16 * cap

    def routing():
        lane_of = lax.broadcasted_iota(jnp.int32, (16, ext), 1)
        row_of = lax.broadcasted_iota(jnp.int32, (16, ext), 0)
        chosen = jnp.where(lane_of == me + row_of * devices, 1.0, 0.0)
        chosen = jnp.where(row_of < 2, chosen, 0.0).astype(jnp.bfloat16)
        column = lax.broadcasted_iota(jnp.int32, (tokens, 1), 0)
        token = lax.broadcasted_iota(jnp.int32, (1, tokens), 1)
        slot = lax.broadcasted_iota(jnp.int32, (slots, 1), 0)
        owner, slot_owner = token // seqs, slot // cap
        slot_rank = slot - slot_owner * cap
        earlier = jnp.where((column // seqs == owner) & (column < token), 1.0, 0.0).astype(jnp.bfloat16)
        for group in range(groups):
            table = xg[pl.ds(16 * group, 16), :, pl.ds(0, ext)].reshape(tokens, ext)
            both = lax.dot_general(chosen, table, (((1,), (1,)), ((), ())), preferred_element_type=jnp.float32)
            named = jnp.where(both > 0.0, 1.0, 0.0)
            rank = jnp.dot(named.astype(jnp.bfloat16), earlier, preferred_element_type=jnp.float32)[0:1].astype(jnp.int32)
            weight = both[0:1] + both[1:2]
            hit = (slot_owner == owner) & (slot_rank == rank) & (named[0:1] > 0.0)
            one = jnp.where(hit, 1.0, 0.0)
            share[pl.ds(group * slots, slots), :] = jnp.broadcast_to(
                jnp.sum(one * weight, axis=1, keepdims=True), (slots, 128)
            )
            pick[group] = one.astype(jnp.bfloat16)
            place[group] = one.T.astype(jnp.bfloat16)

    tile = 256
    total = groups * slots

    def up_chunk(chunk, first):
        here = pl.ds(ext + chunk * CHUNK, CHUNK)
        for group in range(groups):
            x = xg[pl.ds(16 * group, 16), :, here].reshape(tokens, CHUNK)
            xc[pl.ds(group * slots, slots), :] = jnp.dot(
                pick[group], x, preferred_element_type=jnp.float32
            ).astype(jnp.bfloat16)
        for load in weight_loads[chunk]:
            load.wait()

        def body(n, carry):
            at = pl.ds(pl.multiple_of(n * tile, tile), tile)
            for acc, w in ((gacc, wg), (uacc, wu)):
                part = jnp.dot(xc[...], w[pl.ds(chunk * CHUNK, CHUNK), at], preferred_element_type=jnp.float32)
                acc[:, at] = part if first else acc[:, at] + part
            return carry

        lax.fori_loop(0, gacc.shape[1] // tile, body, 0)

    def down_chunk(chunk):
        down_loads[chunk].wait()

        def body(n, carry):
            at = pl.ds(pl.multiple_of(chunk * CHUNK + n * tile, tile), tile)
            to = pl.ds(pl.multiple_of(ext + chunk * CHUNK + n * tile, 128), tile)
            out = jnp.dot(units[...], wd[:, at], preferred_element_type=jnp.float32)
            out = (out * share[:, 0:1]).astype(jnp.bfloat16)
            for group in range(groups):
                y = jnp.dot(place[group], out[group * slots : (group + 1) * slots], preferred_element_type=jnp.float32)
                xg[pl.ds(16 * group, 16), :, to] = y.astype(jnp.bfloat16).reshape(16, seqs, tile)
            return carry

        lax.fori_loop(0, CHUNK // tile, body, 0)

    group_of = min(4, seqs)

    def attend(first):
        own = range(first, first + group_of)
        scored = [jnp.dot(qv[i], kv[i], preferred_element_type=jnp.float32) * SCALE for i in own]
        slot = lax.broadcasted_iota(jnp.int32, scored[0].shape, 1)
        visible = [slot < len_ref[i] for i in own]
        scored = [jnp.where(seen, each, -1e30) for seen, each in zip(visible, scored)]
        top = [jnp.max(each, axis=-1, keepdims=True) for each in scored]
        numer = [jnp.where(seen, jnp.exp(each - most), 0.0) for seen, each, most in zip(visible, scored, top)]
        total = [jnp.sum(each, axis=-1, keepdims=True) for each in numer]
        prob = [(each / whole).astype(jnp.bfloat16) for each, whole in zip(numer, total)]
        for i, each in zip(own, prob):
            ctx[i] = lax.dot_general(
                each, kv[i, pl.ds(0, LATENT), :], (((1,), (1,)), ((), ())), preferred_element_type=jnp.float32
            ).astype(jnp.bfloat16)

    widths = [CHUNK] * chunks + [ext]
    steps, _ = schedule(bits, orders, widths, False, seqs // group_of)
    first_up = True
    for number, (kind, which, step) in enumerate(steps):
        if kind == "hop":
            if step > 0:
                gather_wait(which, step - 1, gr_sem)
            if step < stages:
                gather_start(which, step)
            elif which == chunks:
                routing()
        elif kind == "work":
            up_chunk(which, first_up)
            first_up = False
        else:
            if which == 0:
                for load in loads:
                    load.wait()
            attend(which * group_of)
        if number == chunks:
            for pair in weight_loads:
                for load in pair:
                    load.start()
            for load in down_loads:
                load.start()
    ctx_out = pltpu.make_async_copy(ctx, ctx_hbm, a_sem.at[2])
    ctx_out.start()

    def act(n, carry):
        at = pl.ds(pl.multiple_of(n * tile, tile), tile)
        gate = gacc[:, at]
        units[:, at] = (gate / (1.0 + jnp.exp(-gate)) * uacc[:, at]).astype(jnp.bfloat16)
        return carry

    lax.fori_loop(0, gacc.shape[1] // tile, act, 0)
    for chunk in range(chunks + 1):
        for stage in range(stages):
            gather_wait(chunk, stage, gs_sem)

    def halves(chunk, stage):
        held = held_before(orders[chunk], stage)
        if stage < stages - 1:
            return [(stage, 1 << stage, held)]
        bit = 1 << orders[chunk][stage - 1]
        near, far = [slot for slot in held if slot & bit], [slot for slot in held if not slot & bit]
        return [(stage, 1 << stage, near), (stages, (1 << stage) + len(near), far)]

    def scatter_start(chunk, stage):
        bit = orders[chunk][stage]
        for sem, at, part in halves(chunk, stage):
            for first, count in runs_of(part):
                pltpu.make_async_remote_copy(
                    src_ref=xg.at[pl.ds(first + (1 << bit), count), :, pl.ds(ext + chunk * CHUNK, CHUNK)],
                    dst_ref=got.at[pl.ds(at, count), :, pl.ds(chunk * CHUNK, CHUNK)],
                    send_sem=ss_sem.at[chunk, sem], recv_sem=sr_sem.at[chunk, sem],
                    device_id=partner(bit), device_id_type=MESH,
                ).start()
                at += count

    def scatter_wait(chunk, sem, at, count, sems):
        view = got.at[pl.ds(at, count), :, pl.ds(chunk * CHUNK, CHUNK)]
        pltpu.make_async_copy(view, view, sems.at[chunk, sem]).wait()

    def add(chunk, at, part):
        here, there = pl.ds(ext + chunk * CHUNK, CHUNK), pl.ds(chunk * CHUNK, CHUNK)

        def one(slot, place):
            both = xg[slot, :, here].astype(jnp.float32) + got[place, :, there].astype(jnp.float32)
            xg[slot, :, here] = both.astype(jnp.bfloat16)

        for first, count in runs_of(part):
            if count <= 4:
                for i in range(count):
                    one(first + i, at + i)
            else:

                def body(n, carry, first=first, at=at):
                    for i in range(4):
                        one(first + 4 * n + i, at + 4 * n + i)
                    return carry

                lax.fori_loop(0, count // 4, body, 0)
            at += count

    steps, _ = schedule(bits, orders[:chunks], [CHUNK] * chunks, True, 0)
    for kind, chunk, step in steps:
        if kind == "work":
            down_chunk(chunk)
            continue
        parts = halves(chunk, stages - step) if step > 0 else []
        for number, (sem, at, part) in enumerate(parts):
            scatter_wait(chunk, sem, at, len(part), sr_sem)
            if step < stages:
                add(chunk, at, part)
            if number == 0 and step < stages:
                scatter_start(chunk, stages - 1 - step)
        if step == 0:
            scatter_start(chunk, stages - 1)
        if step == stages:
            here, there = pl.ds(ext + chunk * CHUNK, CHUNK), pl.ds(chunk * CHUNK, CHUNK)
            both = xg[0, :, here].astype(jnp.float32) + got[1, :, there].astype(jnp.float32)
            mix_ref[:, there] = both.astype(jnp.bfloat16)
    for chunk in range(chunks):
        for stage in range(stages):
            for sem, at, part in halves(chunk, stage):
                scatter_wait(chunk, sem, at, len(part), ss_sem)
    ctx_out.wait()


def shards(rows, cols, hidden, route_ids, route_scores, gate_weight, up_weight, down_weight, queries, cache, lengths):
    seqs, width = hidden.shape
    hidden_units = gate_weight.shape[2]
    devices = rows * cols
    cap = max(2, 2 * seqs * route_ids.shape[1] // devices)
    ext = -(-2 * devices // 128) * 128
    bits = bits_of(rows, cols)
    stages = len(bits)
    z = [i for i, bit in enumerate(bits) if bit[0] == "z"]
    y = [i for i, bit in enumerate(bits) if bit[0] == "y"]
    x = [i for i, bit in enumerate(bits) if bit[0] == "x"]
    core = [stages - 1]
    chunks = width // CHUNK
    orders = [z + x + y, y + x + z, z + y + x, z + x + y, x + y + z, z + y + x, z + x + y]
    orders = [orders[i % len(orders)] + core for i in range(chunks)] + [z + y + x + core]
    groups = devices // 16
    slots = groups * 16 * cap
    sems = pltpu.SemaphoreType.DMA((chunks + 1, stages + 1))
    vmem = pl.BlockSpec(memory_space=pltpu.VMEM)
    hbm = pl.BlockSpec(memory_space=pl.ANY)
    bf16, f32 = jnp.bfloat16, jnp.float32
    return pl.pallas_call(
        functools.partial(kernel, (bits, orders, ext, cap, rows, cols)),
        out_shape=(
            jax.ShapeDtypeStruct((seqs, width), bf16),
            jax.ShapeDtypeStruct(queries.shape[:2] + (LATENT,), bf16),
        ),
        in_specs=[vmem, vmem, pl.BlockSpec(memory_space=pltpu.SMEM), vmem, hbm, hbm, hbm, hbm, hbm],
        out_specs=(vmem, hbm),
        scratch_shapes=[
            pltpu.VMEM((devices, seqs, ext + width), bf16),
            pltpu.VMEM((devices, seqs, width), bf16),
            pltpu.VMEM(gate_weight.shape[1:], bf16),
            pltpu.VMEM(up_weight.shape[1:], bf16),
            pltpu.VMEM(down_weight.shape[1:], bf16),
            pltpu.VMEM(queries.shape, bf16),
            pltpu.VMEM(cache.shape[:1] + cache.shape[:0:-1], bf16),
            pltpu.VMEM(queries.shape[:2] + (LATENT,), bf16),
            pltpu.VMEM((groups, 16 * cap, 16 * seqs), bf16),
            pltpu.VMEM((groups, 16 * seqs, 16 * cap), bf16),
            pltpu.VMEM((slots, 128), f32),
            pltpu.VMEM((slots, CHUNK), bf16),
            pltpu.VMEM((slots, hidden_units), f32),
            pltpu.VMEM((slots, hidden_units), f32),
            pltpu.VMEM((slots, hidden_units), bf16),
            sems, sems, sems, sems,
            pltpu.SemaphoreType.DMA((3, chunks)),
            pltpu.SemaphoreType.DMA((3,)),
        ],
        compiler_params=pltpu.CompilerParams(
            collective_id=0, has_side_effects=True, vmem_limit_bytes=62 * 1024 * 1024
        ),
    )(
        route_ids.T, route_scores.T, lengths, hidden, gate_weight, up_weight, down_weight, queries, jnp.swapaxes(cache, 1, 2)
    )


def solution(mesh):
    both = ("row", "col")
    flat, deep = P(both, None), P(both, None, None)
    return jax.shard_map(
        functools.partial(shards, mesh.shape["row"], mesh.shape["col"]),
        mesh=mesh,
        in_specs=(flat, flat, flat, deep, deep, deep, deep, deep, P(both)),
        out_specs=(flat, deep),
        check_vma=False,
    )
```

```python
import functools

import jax
import jax.numpy as jnp
from jax import lax
from jax.experimental import pallas as pl
from jax.experimental.pallas import tpu as pltpu
from jax.sharding import PartitionSpec as P

MESH = pl.DeviceIdType.MESH
LATENT = 512
SCALE = 192 ** (-0.5)
DEPTH = 4
CHUNK = 512
HOP, BLOCK, WORK, FILL, FILL_FROM = 1.5, 0.36, 0.9, 1.5, 2.0


def bits_of(rows, cols):
    tall = cols // DEPTH
    bits = {"z": [], "y": [], "x": []}
    for axis, size, mesh_axis, stride in (("z", DEPTH, "col", tall), ("y", tall, "col", 1), ("x", rows // 2, "row", 2)):
        step = size // 2
        while step >= 1:
            bits[axis].append((axis, mesh_axis, stride * step, step))
            step //= 2
    return bits["z"] + bits["y"] + bits["x"] + [("core", "row", 1, 1 / 4)]


def runs_of(slots):
    runs = []
    for slot in sorted(slots):
        if runs and runs[-1][0] + runs[-1][1] == slot:
            runs[-1][1] += 1
        else:
            runs.append([slot, 1])
    return [tuple(run) for run in runs]


def held_before(order, stage):
    slots = [0]
    for bit in order[:stage]:
        slots += [slot | (1 << bit) for slot in slots]
    return sorted(slots)


def schedule(bits, orders, widths, backward, fillers):
    stages = len(bits)
    clock, free, out = 0.0, {}, []
    hops = [] if backward else [(0.0, chunk, 0) for chunk in range(len(orders))]
    if not backward:
        hops[-1] = (-1.0, len(orders) - 1, 0)
    work = list(range(len(orders))) if backward else []
    fill = list(range(fillers))
    table = backward
    while hops or work or fill:
        hops.sort()
        due = hops[0][0] if hops else float("inf")
        if due > clock + 0.2 and ((work and table) or (fill and clock > FILL_FROM)):
            if work and table:
                chunk = work.pop(0)
                out.append(("work", chunk, 0))
                clock += WORK
                if backward:
                    hops.append((clock, chunk, 0))
            else:
                out.append(("fill", fill.pop(0), 0))
                clock += FILL
            continue
        if not hops:
            clock += 0.5
            continue
        _, chunk, step = hops.pop(0)
        clock = max(clock, due) + 0.1
        out.append(("hop", chunk, step))
        if step > 0 and backward:
            clock += 0.02 * (1 << (stages - step))
        if step == stages:
            if widths[chunk] != CHUNK:
                table = True
                clock += 1.0
            elif not backward:
                work.append(chunk)
            continue
        stage = stages - 1 - step if backward else step
        link = orders[chunk][stage]
        axis, distance = bits[link][0], bits[link][3]
        start = max(clock, free.get(axis, 0.0))
        load = (1 << stage) * widths[chunk] / CHUNK * BLOCK
        end = start + load * distance
        free[axis] = start + load * min(distance, 1)
        hops.append((end + HOP, chunk, step + 1))
    return out, clock


def kernel(
    plan,
    ids_ref, scores_ref, len_ref, hidden_ref, wg_hbm, wu_hbm, wd_hbm, q_hbm, kv_hbm,
    mix_ref, ctx_hbm,
    xg, got, wg, wu, wd, qv, kv, ctx, pick, place, share, xc, gacc, uacc, units,
    gs_sem, gr_sem, ss_sem, sr_sem, w_sem, a_sem,
):
    bits, orders, ext, cap, rows, cols = plan
    stages, chunks = len(bits), len(orders) - 1
    seqs, width = hidden_ref.shape
    devices = rows * cols
    row, col = lax.axis_index("row"), lax.axis_index("col")
    me = row * cols + col

    def partner(bit):
        _, mesh_axis, stride, _ = bits[bit]
        own = row if mesh_axis == "row" else col
        other = own + stride * (1 - 2 * lax.rem(lax.div(own, stride), 2))
        return (other, col) if mesh_axis == "row" else (row, other)

    barrier = pltpu.get_barrier_semaphore()
    for bit in range(stages):
        pl.semaphore_signal(barrier, inc=1, device_id=partner(bit), device_id_type=MESH)

    loads = [
        pltpu.make_async_copy(q_hbm, qv, a_sem.at[0]),
        pltpu.make_async_copy(kv_hbm, kv, a_sem.at[1]),
    ]
    for load in loads:
        load.start()
    weight_loads = []
    for chunk in range(chunks):
        part = pl.ds(chunk * CHUNK, CHUNK)
        weight_loads.append((
            pltpu.make_async_copy(wg_hbm.at[0, part], wg.at[part], w_sem.at[0, chunk]),
            pltpu.make_async_copy(wu_hbm.at[0, part], wu.at[part], w_sem.at[1, chunk]),
        ))
    down_loads = [
        pltpu.make_async_copy(
            wd_hbm.at[0, :, pl.ds(chunk * CHUNK, CHUNK)], wd.at[:, pl.ds(chunk * CHUNK, CHUNK)], w_sem.at[2, chunk]
        )
        for chunk in range(chunks)
    ]

    scores = scores_ref[...]
    combine = 2.5 * scores / jnp.sum(scores, axis=0, keepdims=True)
    ids = ids_ref[...]
    square = (seqs, seqs)
    diagonal = lax.broadcasted_iota(jnp.int32, square, 0) == lax.broadcasted_iota(jnp.int32, square, 1)
    lane = lax.broadcasted_iota(jnp.int32, (seqs, ext), 1)
    table = jnp.zeros((seqs, ext), jnp.float32)
    for k in range(ids.shape[0]):
        weight = jnp.sum(jnp.where(diagonal, combine[k : k + 1], 0.0), axis=1, keepdims=True)
        expert = jnp.sum(jnp.where(diagonal, ids[k : k + 1].astype(jnp.float32), 0.0), axis=1, keepdims=True)
        expert = expert.astype(jnp.int32)
        high = weight.astype(jnp.bfloat16).astype(jnp.float32)
        table += jnp.where(lane == expert, high, 0.0) + jnp.where(lane == expert + devices, weight - high, 0.0)
    xg[0, :, pl.ds(0, ext)] = table.astype(jnp.bfloat16)
    xg[0, :, pl.ds(ext, width)] = hidden_ref[...]
    pl.semaphore_wait(barrier, stages)

    def columns(chunk):
        return pl.ds(0, ext) if chunk == chunks else pl.ds(ext + chunk * CHUNK, CHUNK)

    def gather_start(chunk, stage):
        order = orders[chunk]
        held = held_before(order, stage)
        fresh = sorted(set(held) - set(held_before(order, stage - 1))) if stage else held
        hops = [(stage, held)] if stage < stages - 1 else []
        for to, sent in hops + [(stages - 1, fresh)]:
            for first, count in runs_of(sent):
                pltpu.make_async_remote_copy(
                    src_ref=xg.at[pl.ds(first, count), :, columns(chunk)],
                    dst_ref=xg.at[pl.ds(first + (1 << order[to]), count), :, columns(chunk)],
                    send_sem=gs_sem.at[chunk, to], recv_sem=gr_sem.at[chunk, to],
                    device_id=partner(order[to]), device_id_type=MESH,
                ).start()

    def gather_wait(chunk, stage, sem):
        view = xg.at[pl.ds(0, 1 << stage), :, columns(chunk)]
        pltpu.make_async_copy(view, view, sem.at[chunk, stage]).wait()

    groups = devices // 16
    tokens = 16 * seqs
    slots = 16 * cap

    def routing():
        lane_of = lax.broadcasted_iota(jnp.int32, (16, ext), 1)
        row_of = lax.broadcasted_iota(jnp.int32, (16, ext), 0)
        chosen = jnp.where(lane_of == me + row_of * devices, 1.0, 0.0)
        chosen = jnp.where(row_of < 2, chosen, 0.0).astype(jnp.bfloat16)
        column = lax.broadcasted_iota(jnp.int32, (tokens, 1), 0)
        token = lax.broadcasted_iota(jnp.int32, (1, tokens), 1)
        slot = lax.broadcasted_iota(jnp.int32, (slots, 1), 0)
        owner, slot_owner = token // seqs, slot // cap
        slot_rank = slot - slot_owner * cap
        earlier = jnp.where((column // seqs == owner) & (column < token), 1.0, 0.0).astype(jnp.bfloat16)
        for group in range(groups):
            table = xg[pl.ds(16 * group, 16), :, pl.ds(0, ext)].reshape(tokens, ext)
            both = lax.dot_general(chosen, table, (((1,), (1,)), ((), ())), preferred_element_type=jnp.float32)
            named = jnp.where(both > 0.0, 1.0, 0.0)
            rank = jnp.dot(named.astype(jnp.bfloat16), earlier, preferred_element_type=jnp.float32)[0:1].astype(jnp.int32)
            weight = both[0:1] + both[1:2]
            hit = (slot_owner == owner) & (slot_rank == rank) & (named[0:1] > 0.0)
            one = jnp.where(hit, 1.0, 0.0)
            share[pl.ds(group * slots, slots), :] = jnp.broadcast_to(
                jnp.sum(one * weight, axis=1, keepdims=True), (slots, 128)
            )
            pick[group] = one.astype(jnp.bfloat16)
            place[group] = one.T.astype(jnp.bfloat16)

    tile = 256
    total = groups * slots

    def up_chunk(chunk, first):
        here = pl.ds(ext + chunk * CHUNK, CHUNK)
        for group in range(groups):
            x = xg[pl.ds(16 * group, 16), :, here].reshape(tokens, CHUNK)
            xc[pl.ds(group * slots, slots), :] = jnp.dot(
                pick[group], x, preferred_element_type=jnp.float32
            ).astype(jnp.bfloat16)
        for load in weight_loads[chunk]:
            load.wait()

        def body(n, carry):
            at = pl.ds(pl.multiple_of(n * tile, tile), tile)
            for acc, w in ((gacc, wg), (uacc, wu)):
                part = jnp.dot(xc[...], w[pl.ds(chunk * CHUNK, CHUNK), at], preferred_element_type=jnp.float32)
                acc[:, at] = part if first else acc[:, at] + part
            return carry

        lax.fori_loop(0, gacc.shape[1] // tile, body, 0)

    def down_chunk(chunk):
        down_loads[chunk].wait()

        def body(n, carry):
            at = pl.ds(pl.multiple_of(chunk * CHUNK + n * tile, tile), tile)
            to = pl.ds(pl.multiple_of(ext + chunk * CHUNK + n * tile, 128), tile)
            out = jnp.dot(units[...], wd[:, at], preferred_element_type=jnp.float32)
            out = (out * share[:, 0:1]).astype(jnp.bfloat16)
            for group in range(groups):
                y = jnp.dot(place[group], out[group * slots : (group + 1) * slots], preferred_element_type=jnp.float32)
                xg[pl.ds(16 * group, 16), :, to] = y.astype(jnp.bfloat16).reshape(16, seqs, tile)
            return carry

        lax.fori_loop(0, CHUNK // tile, body, 0)

    group_of = min(4, seqs)

    def attend(first):
        own = range(first, first + group_of)
        scored = [jnp.dot(qv[i], kv[i], preferred_element_type=jnp.float32) * SCALE for i in own]
        slot = lax.broadcasted_iota(jnp.int32, scored[0].shape, 1)
        visible = [slot < len_ref[i] for i in own]
        scored = [jnp.where(seen, each, -1e30) for seen, each in zip(visible, scored)]
        top = [jnp.max(each, axis=-1, keepdims=True) for each in scored]
        numer = [jnp.where(seen, jnp.exp(each - most), 0.0) for seen, each, most in zip(visible, scored, top)]
        total = [jnp.sum(each, axis=-1, keepdims=True) for each in numer]
        prob = [(each / whole).astype(jnp.bfloat16) for each, whole in zip(numer, total)]
        for i, each in zip(own, prob):
            ctx[i] = lax.dot_general(
                each, kv[i, pl.ds(0, LATENT), :], (((1,), (1,)), ((), ())), preferred_element_type=jnp.float32
            ).astype(jnp.bfloat16)

    widths = [CHUNK] * chunks + [ext]
    steps, _ = schedule(bits, orders, widths, False, seqs // group_of)
    needed = [which for kind, which, _ in steps if kind == "work"]
    pending = [weight_loads[which] for which in needed] + [(load,) for load in down_loads]
    before_work = [kind == "work" for kind, _, _ in steps].index(True)
    early = sum(kind == "hop" for kind, _, _ in steps[:before_work]) - chunks - 1
    spread = max(1, early // chunks)
    hops = 0
    first_up = True
    for kind, which, step in steps:
        if kind == "hop":
            if step > 0:
                gather_wait(which, step - 1, gr_sem)
            if step < stages:
                gather_start(which, step)
            elif which == chunks:
                routing()
        elif kind == "work":
            while len(pending) >= 2 * chunks - needed.index(which):
                for load in pending.pop(0):
                    load.start()
            up_chunk(which, first_up)
            first_up = False
        else:
            if which == 0:
                for load in loads:
                    load.wait()
            attend(which * group_of)
        if kind == "hop":
            hops += 1
            if hops > chunks + 1 and pending and (hops - chunks) % spread == 0:
                for load in pending.pop(0):
                    load.start()
    for rest in pending:
        for load in rest:
            load.start()
    ctx_out = pltpu.make_async_copy(ctx, ctx_hbm, a_sem.at[2])
    ctx_out.start()

    def act(n, carry):
        at = pl.ds(pl.multiple_of(n * tile, tile), tile)
        gate = gacc[:, at]
        units[:, at] = (gate / (1.0 + jnp.exp(-gate)) * uacc[:, at]).astype(jnp.bfloat16)
        return carry

    lax.fori_loop(0, gacc.shape[1] // tile, act, 0)
    for chunk in range(chunks + 1):
        for stage in range(stages):
            gather_wait(chunk, stage, gs_sem)

    def halves(chunk, stage):
        held = held_before(orders[chunk], stage)
        if stage < stages - 1:
            return [(stage, 1 << stage, held)]
        bit = 1 << orders[chunk][stage - 1]
        near, far = [slot for slot in held if slot & bit], [slot for slot in held if not slot & bit]
        return [(stage, 1 << stage, near), (stages, (1 << stage) + len(near), far)]

    def scatter_start(chunk, stage):
        bit = orders[chunk][stage]
        for sem, at, part in halves(chunk, stage):
            for first, count in runs_of(part):
                pltpu.make_async_remote_copy(
                    src_ref=xg.at[pl.ds(first + (1 << bit), count), :, pl.ds(ext + chunk * CHUNK, CHUNK)],
                    dst_ref=got.at[pl.ds(at, count), :, pl.ds(chunk * CHUNK, CHUNK)],
                    send_sem=ss_sem.at[chunk, sem], recv_sem=sr_sem.at[chunk, sem],
                    device_id=partner(bit), device_id_type=MESH,
                ).start()
                at += count

    def scatter_wait(chunk, sem, at, count, sems):
        view = got.at[pl.ds(at, count), :, pl.ds(chunk * CHUNK, CHUNK)]
        pltpu.make_async_copy(view, view, sems.at[chunk, sem]).wait()

    def add(chunk, at, part):
        here, there = pl.ds(ext + chunk * CHUNK, CHUNK), pl.ds(chunk * CHUNK, CHUNK)

        def one(slot, place):
            both = xg[slot, :, here].astype(jnp.float32) + got[place, :, there].astype(jnp.float32)
            xg[slot, :, here] = both.astype(jnp.bfloat16)

        for first, count in runs_of(part):
            if count <= 4:
                for i in range(count):
                    one(first + i, at + i)
            else:

                def body(n, carry, first=first, at=at):
                    for i in range(4):
                        one(first + 4 * n + i, at + 4 * n + i)
                    return carry

                lax.fori_loop(0, count // 4, body, 0)
            at += count

    steps, _ = schedule(bits, orders[:chunks], [CHUNK] * chunks, True, 0)
    for kind, chunk, step in steps:
        if kind == "work":
            down_chunk(chunk)
            continue
        parts = halves(chunk, stages - step) if step > 0 else []
        for number, (sem, at, part) in enumerate(parts):
            scatter_wait(chunk, sem, at, len(part), sr_sem)
            if step < stages:
                add(chunk, at, part)
            if number == 0 and step < stages:
                scatter_start(chunk, stages - 1 - step)
        if step == 0:
            scatter_start(chunk, stages - 1)
        if step == stages:
            here, there = pl.ds(ext + chunk * CHUNK, CHUNK), pl.ds(chunk * CHUNK, CHUNK)
            both = xg[0, :, here].astype(jnp.float32) + got[1, :, there].astype(jnp.float32)
            mix_ref[:, there] = both.astype(jnp.bfloat16)
    for chunk in range(chunks):
        for stage in range(stages):
            for sem, at, part in halves(chunk, stage):
                scatter_wait(chunk, sem, at, len(part), ss_sem)
    ctx_out.wait()


def shards(rows, cols, hidden, route_ids, route_scores, gate_weight, up_weight, down_weight, queries, cache, lengths):
    seqs, width = hidden.shape
    hidden_units = gate_weight.shape[2]
    devices = rows * cols
    cap = max(2, 2 * seqs * route_ids.shape[1] // devices)
    ext = -(-2 * devices // 128) * 128
    bits = bits_of(rows, cols)
    stages = len(bits)
    z = [i for i, bit in enumerate(bits) if bit[0] == "z"]
    y = [i for i, bit in enumerate(bits) if bit[0] == "y"]
    x = [i for i, bit in enumerate(bits) if bit[0] == "x"]
    core = [stages - 1]
    chunks = width // CHUNK
    orders = [z + x + y, y + x + z, z + y + x, z + x + y, x + y + z, z + y + x, z + x + y]
    orders = [orders[i % len(orders)] + core for i in range(chunks)] + [z + y + x + core]
    groups = devices // 16
    slots = groups * 16 * cap
    sems = pltpu.SemaphoreType.DMA((chunks + 1, stages + 1))
    vmem = pl.BlockSpec(memory_space=pltpu.VMEM)
    hbm = pl.BlockSpec(memory_space=pl.ANY)
    bf16, f32 = jnp.bfloat16, jnp.float32
    return pl.pallas_call(
        functools.partial(kernel, (bits, orders, ext, cap, rows, cols)),
        out_shape=(
            jax.ShapeDtypeStruct((seqs, width), bf16),
            jax.ShapeDtypeStruct(queries.shape[:2] + (LATENT,), bf16),
        ),
        in_specs=[vmem, vmem, pl.BlockSpec(memory_space=pltpu.SMEM), vmem, hbm, hbm, hbm, hbm, hbm],
        out_specs=(vmem, hbm),
        scratch_shapes=[
            pltpu.VMEM((devices, seqs, ext + width), bf16),
            pltpu.VMEM((devices, seqs, width), bf16),
            pltpu.VMEM(gate_weight.shape[1:], bf16),
            pltpu.VMEM(up_weight.shape[1:], bf16),
            pltpu.VMEM(down_weight.shape[1:], bf16),
            pltpu.VMEM(queries.shape, bf16),
            pltpu.VMEM(cache.shape[:1] + cache.shape[:0:-1], bf16),
            pltpu.VMEM(queries.shape[:2] + (LATENT,), bf16),
            pltpu.VMEM((groups, 16 * cap, 16 * seqs), bf16),
            pltpu.VMEM((groups, 16 * seqs, 16 * cap), bf16),
            pltpu.VMEM((slots, 128), f32),
            pltpu.VMEM((slots, CHUNK), bf16),
            pltpu.VMEM((slots, hidden_units), f32),
            pltpu.VMEM((slots, hidden_units), f32),
            pltpu.VMEM((slots, hidden_units), bf16),
            sems, sems, sems, sems,
            pltpu.SemaphoreType.DMA((3, chunks)),
            pltpu.SemaphoreType.DMA((3,)),
        ],
        compiler_params=pltpu.CompilerParams(
            collective_id=0, has_side_effects=True, vmem_limit_bytes=62 * 1024 * 1024
        ),
    )(
        route_ids.T, route_scores.T, lengths, hidden, gate_weight, up_weight, down_weight, queries, jnp.swapaxes(cache, 1, 2)
    )


def solution(mesh):
    both = ("row", "col")
    flat, deep = P(both, None), P(both, None, None)
    return jax.shard_map(
        functools.partial(shards, mesh.shape["row"], mesh.shape["col"]),
        mesh=mesh,
        in_specs=(flat, flat, flat, deep, deep, deep, deep, deep, P(both)),
        out_specs=(flat, deep),
        check_vma=False,
    )
```

```python
import functools

import jax
import jax.numpy as jnp
from jax import lax
from jax.experimental import pallas as pl
from jax.experimental.pallas import tpu as pltpu
from jax.sharding import PartitionSpec as P

MESH = pl.DeviceIdType.MESH
LATENT = 512
SCALE = 192 ** (-0.5)
DEPTH = 4
CHUNK = 896
HOP, BLOCK, WORK, FILL, FILL_FROM = 1.0, 0.65, 1.5, 1.5, 2.0


def bits_of(rows, cols):
    tall = cols // DEPTH
    bits = {"z": [], "y": [], "x": []}
    for axis, size, mesh_axis, stride in (("z", DEPTH, "col", tall), ("y", tall, "col", 1), ("x", rows // 2, "row", 2)):
        step = size // 2
        while step >= 1:
            bits[axis].append((axis, mesh_axis, stride * step, step))
            step //= 2
    return bits["z"] + bits["y"] + bits["x"] + [("core", "row", 1, 1 / 6)]


def runs_of(slots):
    runs = []
    for slot in sorted(slots):
        if runs and runs[-1][0] + runs[-1][1] == slot:
            runs[-1][1] += 1
        else:
            runs.append([slot, 1])
    return [tuple(run) for run in runs]


def held_before(order, stage):
    slots = [0]
    for bit in order[:stage]:
        slots += [slot | (1 << bit) for slot in slots]
    return sorted(slots)


def schedule(bits, orders, widths, backward, fillers):
    stages = len(bits)
    clock, free, out = 0.0, {}, []
    hops = [] if backward else [(0.0, chunk, 0) for chunk in range(len(orders))]
    if not backward:
        hops[-1] = (-1.0, len(orders) - 1, 0)
    work = list(range(len(orders))) if backward else []
    fill = list(range(fillers))
    table = backward
    while hops or work or fill:
        hops.sort()
        due = hops[0][0] if hops else float("inf")
        if due > clock + 0.2 and ((work and table) or (fill and clock > FILL_FROM)):
            if work and table:
                chunk = work.pop(0)
                out.append(("work", chunk, 0))
                clock += WORK
                if backward:
                    hops.append((clock, chunk, 0))
            else:
                out.append(("fill", fill.pop(0), 0))
                clock += FILL
            continue
        if not hops:
            clock += 0.5
            continue
        _, chunk, step = hops.pop(0)
        clock = max(clock, due) + 0.1
        out.append(("hop", chunk, step))
        if step > 0 and backward:
            clock += 0.02 * (1 << (stages - step))
        if step == stages:
            if widths[chunk] != CHUNK:
                table = True
                clock += 1.0
            elif not backward:
                work.append(chunk)
            continue
        stage = stages - 1 - step if backward else step
        link = orders[chunk][stage]
        axis, distance = bits[link][0], bits[link][3]
        start = max(clock, free.get(axis, 0.0))
        load = (1 << stage) * widths[chunk] / CHUNK * BLOCK
        end = start + load * distance
        free[axis] = start + load * min(distance, 1)
        hops.append((end + HOP, chunk, step + 1))
    return out, clock


def kernel(
    plan,
    ids_ref, scores_ref, len_ref, hidden_ref, wg_hbm, wu_hbm, wd_hbm, q_hbm, kv_hbm,
    mix_ref, ctx_hbm,
    xg, got, wg, wu, wd, qv, kv, ctx, pick, place, share, xc, gacc, uacc, units,
    gs_sem, gr_sem, ss_sem, sr_sem, w_sem, a_sem,
):
    bits, orders, ext, cap, rows, cols = plan
    stages, chunks = len(bits), len(orders) - 1
    seqs, width = hidden_ref.shape
    devices = rows * cols
    row, col = lax.axis_index("row"), lax.axis_index("col")
    me = row * cols + col

    def partner(bit):
        _, mesh_axis, stride, _ = bits[bit]
        own = row if mesh_axis == "row" else col
        other = own + stride * (1 - 2 * lax.rem(lax.div(own, stride), 2))
        return (other, col) if mesh_axis == "row" else (row, other)

    barrier = pltpu.get_barrier_semaphore()
    for bit in range(stages):
        pl.semaphore_signal(barrier, inc=1, device_id=partner(bit), device_id_type=MESH)

    loads = [
        pltpu.make_async_copy(q_hbm, qv, a_sem.at[0]),
        pltpu.make_async_copy(kv_hbm, kv, a_sem.at[1]),
    ]
    for load in loads:
        load.start()
    weight_loads = []
    for chunk in range(chunks):
        part = pl.ds(chunk * CHUNK, CHUNK)
        weight_loads.append((
            pltpu.make_async_copy(wg_hbm.at[0, part], wg.at[part], w_sem.at[0, chunk]),
            pltpu.make_async_copy(wu_hbm.at[0, part], wu.at[part], w_sem.at[1, chunk]),
        ))
    down_loads = [
        pltpu.make_async_copy(
            wd_hbm.at[0, :, pl.ds(chunk * CHUNK, CHUNK)], wd.at[:, pl.ds(chunk * CHUNK, CHUNK)], w_sem.at[2, chunk]
        )
        for chunk in range(chunks)
    ]

    scores = scores_ref[...]
    combine = 2.5 * scores / jnp.sum(scores, axis=0, keepdims=True)
    ids = ids_ref[...]
    square = (seqs, seqs)
    diagonal = lax.broadcasted_iota(jnp.int32, square, 0) == lax.broadcasted_iota(jnp.int32, square, 1)
    lane = lax.broadcasted_iota(jnp.int32, (seqs, ext), 1)
    table = jnp.zeros((seqs, ext), jnp.float32)
    for k in range(ids.shape[0]):
        weight = jnp.sum(jnp.where(diagonal, combine[k : k + 1], 0.0), axis=1, keepdims=True)
        expert = jnp.sum(jnp.where(diagonal, ids[k : k + 1].astype(jnp.float32), 0.0), axis=1, keepdims=True)
        expert = expert.astype(jnp.int32)
        high = weight.astype(jnp.bfloat16).astype(jnp.float32)
        table += jnp.where(lane == expert, high, 0.0) + jnp.where(lane == expert + devices, weight - high, 0.0)
    xg[0, :, pl.ds(0, ext)] = table.astype(jnp.bfloat16)
    xg[0, :, pl.ds(ext, width)] = hidden_ref[...]
    pl.semaphore_wait(barrier, stages)

    def columns(chunk):
        return pl.ds(0, ext) if chunk == chunks else pl.ds(ext + chunk * CHUNK, CHUNK)

    def gather_start(chunk, stage):
        order = orders[chunk]
        held = held_before(order, stage)
        fresh = sorted(set(held) - set(held_before(order, stage - 1))) if stage else held
        hops = [(stage, held)] if stage < stages - 1 else []
        for to, sent in hops + [(stages - 1, fresh)]:
            for first, count in runs_of(sent):
                pltpu.make_async_remote_copy(
                    src_ref=xg.at[pl.ds(first, count), :, columns(chunk)],
                    dst_ref=xg.at[pl.ds(first + (1 << order[to]), count), :, columns(chunk)],
                    send_sem=gs_sem.at[chunk, to], recv_sem=gr_sem.at[chunk, to],
                    device_id=partner(order[to]), device_id_type=MESH,
                ).start()

    def gather_wait(chunk, stage, sem):
        view = xg.at[pl.ds(0, 1 << stage), :, columns(chunk)]
        pltpu.make_async_copy(view, view, sem.at[chunk, stage]).wait()

    groups = devices // 16
    tokens = 16 * seqs
    slots = 16 * cap

    def routing():
        lane_of = lax.broadcasted_iota(jnp.int32, (16, ext), 1)
        row_of = lax.broadcasted_iota(jnp.int32, (16, ext), 0)
        chosen = jnp.where(lane_of == me + row_of * devices, 1.0, 0.0)
        chosen = jnp.where(row_of < 2, chosen, 0.0).astype(jnp.bfloat16)
        column = lax.broadcasted_iota(jnp.int32, (tokens, 1), 0)
        token = lax.broadcasted_iota(jnp.int32, (1, tokens), 1)
        slot = lax.broadcasted_iota(jnp.int32, (slots, 1), 0)
        owner, slot_owner = token // seqs, slot // cap
        slot_rank = slot - slot_owner * cap
        earlier = jnp.where((column // seqs == owner) & (column < token), 1.0, 0.0).astype(jnp.bfloat16)
        for group in range(groups):
            table = xg[pl.ds(16 * group, 16), :, pl.ds(0, ext)].reshape(tokens, ext)
            both = lax.dot_general(chosen, table, (((1,), (1,)), ((), ())), preferred_element_type=jnp.float32)
            named = jnp.where(both > 0.0, 1.0, 0.0)
            rank = jnp.dot(named.astype(jnp.bfloat16), earlier, preferred_element_type=jnp.float32)[0:1].astype(jnp.int32)
            weight = both[0:1] + both[1:2]
            hit = (slot_owner == owner) & (slot_rank == rank) & (named[0:1] > 0.0)
            one = jnp.where(hit, 1.0, 0.0)
            share[pl.ds(group * slots, slots), :] = jnp.broadcast_to(
                jnp.sum(one * weight, axis=1, keepdims=True), (slots, 128)
            )
            pick[group] = one.astype(jnp.bfloat16)
            place[group] = one.T.astype(jnp.bfloat16)

    tile = 256
    total = groups * slots

    def up_chunk(chunk, first):
        here = pl.ds(ext + chunk * CHUNK, CHUNK)
        for group in range(groups):
            x = xg[pl.ds(16 * group, 16), :, here].reshape(tokens, CHUNK)
            xc[pl.ds(group * slots, slots), :] = jnp.dot(
                pick[group], x, preferred_element_type=jnp.float32
            ).astype(jnp.bfloat16)
        for load in weight_loads[chunk]:
            load.wait()

        def body(n, carry):
            at = pl.ds(pl.multiple_of(n * tile, tile), tile)
            for acc, w in ((gacc, wg), (uacc, wu)):
                part = jnp.dot(xc[...], w[pl.ds(chunk * CHUNK, CHUNK), at], preferred_element_type=jnp.float32)
                acc[:, at] = part if first else acc[:, at] + part
            return carry

        lax.fori_loop(0, gacc.shape[1] // tile, body, 0)

    def down_chunk(chunk):
        down_loads[chunk].wait()

        for start in range(0, CHUNK, tile):
            wide = min(tile, CHUNK - start)
            at, to = pl.ds(chunk * CHUNK + start, wide), pl.ds(ext + chunk * CHUNK + start, wide)
            out = jnp.dot(units[...], wd[:, at], preferred_element_type=jnp.float32)
            out = (out * share[:, 0:1]).astype(jnp.bfloat16)
            for group in range(groups):
                y = jnp.dot(place[group], out[group * slots : (group + 1) * slots], preferred_element_type=jnp.float32)
                xg[pl.ds(16 * group, 16), :, to] = y.astype(jnp.bfloat16).reshape(16, seqs, wide)

    group_of = min(4, seqs)

    def attend(first):
        own = range(first, first + group_of)
        scored = [jnp.dot(qv[i], kv[i], preferred_element_type=jnp.float32) * SCALE for i in own]
        slot = lax.broadcasted_iota(jnp.int32, scored[0].shape, 1)
        visible = [slot < len_ref[i] for i in own]
        scored = [jnp.where(seen, each, -1e30) for seen, each in zip(visible, scored)]
        top = [jnp.max(each, axis=-1, keepdims=True) for each in scored]
        numer = [jnp.where(seen, jnp.exp(each - most), 0.0) for seen, each, most in zip(visible, scored, top)]
        total = [jnp.sum(each, axis=-1, keepdims=True) for each in numer]
        prob = [(each / whole).astype(jnp.bfloat16) for each, whole in zip(numer, total)]
        for i, each in zip(own, prob):
            ctx[i] = lax.dot_general(
                each, kv[i, pl.ds(0, LATENT), :], (((1,), (1,)), ((), ())), preferred_element_type=jnp.float32
            ).astype(jnp.bfloat16)

    widths = [CHUNK] * chunks + [ext]
    steps, _ = schedule(bits, orders, widths, False, seqs // group_of)
    first_up = True
    for number, (kind, which, step) in enumerate(steps):
        if kind == "hop":
            if step > 0:
                gather_wait(which, step - 1, gr_sem)
            if step < stages:
                gather_start(which, step)
            elif which == chunks:
                routing()
        elif kind == "work":
            up_chunk(which, first_up)
            first_up = False
        else:
            if which == 0:
                for load in loads:
                    load.wait()
            attend(which * group_of)
        if number == chunks:
            for pair in weight_loads:
                for load in pair:
                    load.start()
            for load in down_loads:
                load.start()
    ctx_out = pltpu.make_async_copy(ctx, ctx_hbm, a_sem.at[2])
    ctx_out.start()

    def act(n, carry):
        at = pl.ds(pl.multiple_of(n * tile, tile), tile)
        gate = gacc[:, at]
        units[:, at] = (gate / (1.0 + jnp.exp(-gate)) * uacc[:, at]).astype(jnp.bfloat16)
        return carry

    lax.fori_loop(0, gacc.shape[1] // tile, act, 0)
    for chunk in range(chunks + 1):
        for stage in range(stages):
            gather_wait(chunk, stage, gs_sem)

    def halves(chunk, stage):
        held = held_before(orders[chunk], stage)
        if stage < stages - 1:
            return [(stage, 1 << stage, held)]
        bit = 1 << orders[chunk][stage - 1]
        near, far = [slot for slot in held if slot & bit], [slot for slot in held if not slot & bit]
        return [(stage, 1 << stage, near), (stages, (1 << stage) + len(near), far)]

    def scatter_start(chunk, stage):
        bit = orders[chunk][stage]
        for sem, at, part in halves(chunk, stage):
            for first, count in runs_of(part):
                pltpu.make_async_remote_copy(
                    src_ref=xg.at[pl.ds(first + (1 << bit), count), :, pl.ds(ext + chunk * CHUNK, CHUNK)],
                    dst_ref=got.at[pl.ds(at, count), :, pl.ds(chunk * CHUNK, CHUNK)],
                    send_sem=ss_sem.at[chunk, sem], recv_sem=sr_sem.at[chunk, sem],
                    device_id=partner(bit), device_id_type=MESH,
                ).start()
                at += count

    def scatter_wait(chunk, sem, at, count, sems):
        view = got.at[pl.ds(at, count), :, pl.ds(chunk * CHUNK, CHUNK)]
        pltpu.make_async_copy(view, view, sems.at[chunk, sem]).wait()

    def add(chunk, at, part):
        here, there = pl.ds(ext + chunk * CHUNK, CHUNK), pl.ds(chunk * CHUNK, CHUNK)

        def one(slot, place):
            both = xg[slot, :, here].astype(jnp.float32) + got[place, :, there].astype(jnp.float32)
            xg[slot, :, here] = both.astype(jnp.bfloat16)

        for first, count in runs_of(part):
            if count <= 4:
                for i in range(count):
                    one(first + i, at + i)
            else:

                def body(n, carry, first=first, at=at):
                    for i in range(4):
                        one(first + 4 * n + i, at + 4 * n + i)
                    return carry

                lax.fori_loop(0, count // 4, body, 0)
            at += count

    steps, _ = schedule(bits, orders[:chunks], [CHUNK] * chunks, True, 0)
    for kind, chunk, step in steps:
        if kind == "work":
            down_chunk(chunk)
            continue
        parts = halves(chunk, stages - step) if step > 0 else []
        for number, (sem, at, part) in enumerate(parts):
            scatter_wait(chunk, sem, at, len(part), sr_sem)
            if step < stages:
                add(chunk, at, part)
            if number == 0 and step < stages:
                scatter_start(chunk, stages - 1 - step)
        if step == 0:
            scatter_start(chunk, stages - 1)
        if step == stages:
            here, there = pl.ds(ext + chunk * CHUNK, CHUNK), pl.ds(chunk * CHUNK, CHUNK)
            both = xg[0, :, here].astype(jnp.float32) + got[1, :, there].astype(jnp.float32)
            mix_ref[:, there] = both.astype(jnp.bfloat16)
    for chunk in range(chunks):
        for stage in range(stages):
            for sem, at, part in halves(chunk, stage):
                scatter_wait(chunk, sem, at, len(part), ss_sem)
    ctx_out.wait()


def shards(rows, cols, hidden, route_ids, route_scores, gate_weight, up_weight, down_weight, queries, cache, lengths):
    seqs, width = hidden.shape
    hidden_units = gate_weight.shape[2]
    devices = rows * cols
    cap = max(2, 2 * seqs * route_ids.shape[1] // devices)
    ext = -(-2 * devices // 128) * 128
    bits = bits_of(rows, cols)
    stages = len(bits)
    z = [i for i, bit in enumerate(bits) if bit[0] == "z"]
    y = [i for i, bit in enumerate(bits) if bit[0] == "y"]
    x = [i for i, bit in enumerate(bits) if bit[0] == "x"]
    core = [stages - 1]
    chunks = width // CHUNK
    orders = [z + x + y, y + x + z, z + y + x, z + x + y]
    orders = [orders[i % len(orders)] + core for i in range(chunks)] + [z + y + x + core]
    groups = devices // 16
    slots = groups * 16 * cap
    sems = pltpu.SemaphoreType.DMA((chunks + 1, stages + 1))
    vmem = pl.BlockSpec(memory_space=pltpu.VMEM)
    hbm = pl.BlockSpec(memory_space=pl.ANY)
    bf16, f32 = jnp.bfloat16, jnp.float32
    return pl.pallas_call(
        functools.partial(kernel, (bits, orders, ext, cap, rows, cols)),
        out_shape=(
            jax.ShapeDtypeStruct((seqs, width), bf16),
            jax.ShapeDtypeStruct(queries.shape[:2] + (LATENT,), bf16),
        ),
        in_specs=[vmem, vmem, pl.BlockSpec(memory_space=pltpu.SMEM), vmem, hbm, hbm, hbm, hbm, hbm],
        out_specs=(vmem, hbm),
        scratch_shapes=[
            pltpu.VMEM((devices, seqs, ext + width), bf16),
            pltpu.VMEM((devices, seqs, width), bf16),
            pltpu.VMEM(gate_weight.shape[1:], bf16),
            pltpu.VMEM(up_weight.shape[1:], bf16),
            pltpu.VMEM(down_weight.shape[1:], bf16),
            pltpu.VMEM(queries.shape, bf16),
            pltpu.VMEM(cache.shape[:1] + cache.shape[:0:-1], bf16),
            pltpu.VMEM(queries.shape[:2] + (LATENT,), bf16),
            pltpu.VMEM((groups, 16 * cap, 16 * seqs), bf16),
            pltpu.VMEM((groups, 16 * seqs, 16 * cap), bf16),
            pltpu.VMEM((slots, 128), f32),
            pltpu.VMEM((slots, CHUNK), bf16),
            pltpu.VMEM((slots, hidden_units), f32),
            pltpu.VMEM((slots, hidden_units), f32),
            pltpu.VMEM((slots, hidden_units), bf16),
            sems, sems, sems, sems,
            pltpu.SemaphoreType.DMA((3, chunks)),
            pltpu.SemaphoreType.DMA((3,)),
        ],
        compiler_params=pltpu.CompilerParams(
            collective_id=0, has_side_effects=True, vmem_limit_bytes=62 * 1024 * 1024
        ),
    )(
        route_ids.T, route_scores.T, lengths, hidden, gate_weight, up_weight, down_weight, queries, jnp.swapaxes(cache, 1, 2)
    )


def solution(mesh):
    both = ("row", "col")
    flat, deep = P(both, None), P(both, None, None)
    return jax.shard_map(
        functools.partial(shards, mesh.shape["row"], mesh.shape["col"]),
        mesh=mesh,
        in_specs=(flat, flat, flat, deep, deep, deep, deep, deep, P(both)),
        out_specs=(flat, deep),
        check_vma=False,
    )
```
